256 devices in a mesh: row: 8 (over z), col: 32 (over y, x, core).
Axes of the slice: x: 4, y: 4, z: 8, core: 2. Of those that a mesh axis runs over, the one named last changes fastest.
Arguments:
- tokens: bfloat16 [1024, 6144], P('row', 'col'), may hold values from -600 to 600
- norm_gain: float32 [6144], P('col'), may hold values from 0.1 to 1.9
- up_weight: bfloat16 [6144, 24576], P('row', 'col'), may hold values from -0.078125 to 0.078125
- up_bias: float32 [24576], P('col'), may hold values from -3 to 3
- cotangent: bfloat16 [1024, 24576], P('row', 'col'), may hold values from -6 to 6
Outputs:
- activated: bfloat16 [1024, 24576], P('row', 'col')
- input_grad: bfloat16 [1024, 6144], P('row', 'col')
- weight_grad: float32 [6144, 24576], P('row', 'col')
- bias_grad: float32 [24576], P('col')
- gain_grad: float32 [6144], P('col')
The draws below stay inside these ranges and needn't reach their ends.
All inputs are finite; a program needn't handle non-finite values.
Results may differ from the reference program's by a relative error of at most 0.0055.
Values may be sent and summed in bfloat16 or wider, within the bound.
A program may use at most 128 MiB of HBM per device.

```python
import jax
import jax.numpy as jnp
from jax import lax

D = 6144
FF = 24576
TOKENS = 1024


def draw_tokens(key, part):
    key = jax.random.fold_in(key, 11)
    kbase, krow, kcol = jax.random.split(key, 3)
    rowpos = jax.random.uniform(krow, (TOKENS, 1), jnp.float32)
    colpos = jax.random.uniform(kcol, (1, D), jnp.float32)
    ramp = jnp.arange(D, dtype=jnp.float32)[None, :] / D
    colscale = jnp.power(10.0, colpos) * jnp.power(3.0, ramp)
    base = jnp.clip(jax.random.normal(kbase, (TOKENS, D), jnp.float32), -6.0, 6.0)
    rowscale = jnp.power(10.0, rowpos)
    return (0.3 * base * rowscale * colscale).astype(jnp.bfloat16)


def shard_levels(stream_key, dims, cuts, smallest, largest):
    def one(axis_at, parts):
        draws = jax.random.uniform(jax.random.fold_in(jax.random.fold_in(stream_key, 6), axis_at), (parts,), jnp.float32, smallest / len(cuts), largest / len(cuts))
        return jnp.repeat(jnp.exp(draws), dims[axis_at] // parts).reshape((-1,) + (1,) * (len(dims) - axis_at - 1))

    factor_of = one(*cuts[0])
    for cut in cuts[1:]:
        factor_of = factor_of * one(*cut)
    return factor_of


def scatter_about(own_key, shape, width, reach, cuts=(), kind=jnp.bfloat16):
    array = jax.random.normal(own_key, shape, jnp.float32) * width
    if len(cuts) > 0:
        array = shard_levels(own_key, shape, cuts, -0.22, 0.18) * array
    return jnp.clip(array, min=-reach, max=reach).astype(kind)


def setup_inputs(seed: int = 0) -> dict:
    arg_keys = jax.random.split(jax.random.key(seed), 6)
    return {
        "tokens": draw_tokens(jax.random.fold_in(arg_keys[5], 71), 0),
        "norm_gain": jnp.clip(1.0 + 0.18 * jax.random.normal(arg_keys[1], (D,), jnp.float32), 0.1, 1.9),
        "up_weight": scatter_about(arg_keys[2], (D, FF), D ** -0.5, 0.078125, ((0, 8), (1, 32))),
        "up_bias": scatter_about(arg_keys[3], (FF,), 0.5, 3.0, ((0, 32),), jnp.float32),
        "cotangent": scatter_about(arg_keys[4], (TOKENS, FF), 1.0, 6.0, ((0, 8), (1, 32))),
    }


def gelu_exact(value):
    return jax.nn.gelu(value, approximate=False)

def reference(tokens, norm_gain, up_weight, up_bias, cotangent):
    xf = tokens.astype(jnp.float32)
    mean = lax.optimization_barrier(jnp.mean(xf, axis=1, keepdims=True))
    centred = xf - mean
    var = lax.optimization_barrier(jnp.mean(centred * centred, axis=1, keepdims=True))
    rstd = lax.rsqrt(var + 1e-06)
    normed = centred * rstd
    scaled = (normed * norm_gain).astype(jnp.bfloat16)
    pre = jnp.dot(scaled, up_weight, preferred_element_type=jnp.float32) + up_bias
    activated = gelu_exact(pre).astype(jnp.bfloat16)
    _, back = jax.vjp(gelu_exact, pre)
    pre_grad = back(cotangent.astype(jnp.float32))[0].astype(jnp.bfloat16)
    scaled_grad = lax.dot_general(pre_grad, up_weight, (((1,), (1,)), ((), ())), preferred_element_type=jnp.float32)
    gain_grad = lax.optimization_barrier(jnp.sum(scaled_grad * normed, axis=0))
    grads = scaled_grad * norm_gain
    first = lax.optimization_barrier(jnp.mean(grads, axis=1, keepdims=True))
    second = lax.optimization_barrier(jnp.mean(grads * normed, axis=1, keepdims=True))
    input_grad = (rstd * (grads - first - normed * second)).astype(jnp.bfloat16)
    weight_grad = lax.dot_general(scaled, pre_grad, (((0,), (0,)), ((), ())), preferred_element_type=jnp.float32)
    bias_grad = lax.optimization_barrier(jnp.sum(pre_grad.astype(jnp.float32), axis=0))
    return (activated, input_grad, weight_grad, bias_grad, gain_grad)
```

```python
import functools

import jax
import jax.numpy as jnp
from jax import lax
from jax.experimental import pallas as pl
from jax.experimental.pallas import tpu as pltpu
from jax.sharding import PartitionSpec as P

D = 6144
F = 192
T = 128
K = 768
HALF = K // 2
MESH = pl.DeviceIdType.MESH
F32 = jnp.float32
BF16 = jnp.bfloat16
SQRT_HALF = 0.7071067811865476
INV_SQRT_2PI = 0.3989422804014327


def split3(row):
    hi = row.astype(BF16).astype(F32)
    rest = row - hi
    mid = rest.astype(BF16).astype(F32)
    low = rest - mid
    at = lax.broadcasted_iota(jnp.int32, (8, row.shape[1]), 0)
    rows = jnp.where(at == 0, hi, jnp.where(at == 1, mid, jnp.where(at == 2, low, 0.0)))
    return rows.astype(BF16)


def dot_nt(a, b):
    return lax.dot_general(a, b, (((1,), (1,)), ((), ())), preferred_element_type=F32)


def kernel(
    tok_ref, gain_ref, w_ref, bias_ref, cot_ref,
    act_ref, xg_ref, wg_ref, bg_ref, gg_ref,
    chunk, normt, gaint, stat1, stat2, xb, part, pre, pg,
    rs_out, rs_in, ce_out, ce_in, rb_out, rb_in, own, ra_out, ra_in, home_out, home_in,
    wz, gz,
    s1_s, s1_r, s2_s, s2_r, sh_s, sh_r, xa_s, xa_r, xb_s, xb_r, xc_s, xc_r,
    wz_s, wz_r, gz_s, gz_r, rs_s, rs_r, ag_s, ag_r, ce_s, ce_r, rb_s, rb_r, ra_s, ra_r, hm_s, hm_r,
):
    r = lax.axis_index("row")
    c = lax.axis_index("col")
    y = c // 8
    x = (c // 2) % 4
    e = c % 2
    a = (1 - e) * x + e * y
    b = (1 - e) * y + e * x

    def at(z, yy, xx, ee):
        return (z, (yy * 4 + xx) * 2 + ee)

    def place(z, aa, bb, ee):
        return at(z, (1 - ee) * bb + ee * aa, (1 - ee) * aa + ee * bb, ee)

    def zpeer(j):
        return at((r + j) % 8, y, x, e)

    def apeer(j):
        return place(r, (a + j) % 4, b, e)

    def bpeer(j):
        return place(r, a, (b + j) % 4, e)

    core = at(r, y, x, 1 - e)
    my_k = (a + 3) % 4
    my_q = 2 * ((b + 3) % 4) + e
    owner = place(c // 4, (c % 4 + 1) % 4, (r // 2 + 1) % 4, r % 2)
    home = (my_q, 4 * r + my_k)

    peers = [zpeer(j) for j in range(1, 8)]
    peers += [apeer(j) for j in (1, 2, 3)] + [bpeer(j) for j in (1, 2, 3)]
    peers += [core, owner, home]
    barrier = pltpu.get_barrier_semaphore()
    for peer in peers:
        pl.semaphore_signal(barrier, inc=1, device_id=peer, device_id_type=MESH)
    pl.semaphore_wait(barrier, len(peers))

    def send(src, dst, ssem, rsem, to):
        return pltpu.make_async_remote_copy(
            src_ref=src, dst_ref=dst, send_sem=ssem, recv_sem=rsem, device_id=to, device_id_type=MESH
        )

    def arrived(dst, ssem, rsem):
        send(dst, dst, ssem, rsem, core).wait_recv()

    pending = []

    def go(src, dst, ssem, rsem, to):
        copy = send(src, dst, ssem, rsem, to)
        copy.start()
        pending.append(copy)

    def plane_gather(tiles, ssem, rsem):
        mine = (e * 4 + b) * 4
        for j in (1, 2, 3):
            ref = tiles.at[mine + a]
            go(ref, ref, ssem.at[j - 1], rsem.at[j - 1], apeer(j))
        yield
        for j in (1, 2, 3):
            arrived(tiles.at[mine + (a + 4 - j) % 4], ssem.at[j - 1], rsem.at[j - 1])
        for j in (1, 2, 3):
            ref = tiles.at[pl.ds(mine, 4)]
            go(ref, ref, ssem.at[j + 2], rsem.at[j + 2], bpeer(j))
        yield
        for j in (1, 2, 3):
            ref = tiles.at[pl.ds((e * 4 + (b + 4 - j) % 4) * 4, 4)]
            arrived(ref, ssem.at[j + 2], rsem.at[j + 2])
        ref = tiles.at[pl.ds(e * 16, 16)]
        go(ref, ref, ssem.at[6], rsem.at[6], core)
        yield
        arrived(tiles.at[pl.ds((1 - e) * 16, 16)], ssem.at[6], rsem.at[6])
        yield

    xt = tok_ref[...].astype(F32).T
    gaint[...] = jnp.broadcast_to(gain_ref[...], (T, F)).T
    total = jnp.sum(xt, axis=0, keepdims=True)
    dev = xt - total / F
    squares = jnp.sum(dev * dev, axis=0, keepdims=True)
    slot = (e * 4 + b) * 4 + a
    stat1[slot] = jnp.zeros((8, T), F32)
    stat1[slot, 0:1, :] = total
    stat1[slot, 1:2, :] = squares
    stat1[slot, 2:3, :] = gain_ref[:, 0:128]
    stat1[slot, 3:4, 0:64] = gain_ref[:, 128:192]
    for _ in plane_gather(stat1, s1_s, s1_r):
        pass
    sums = stat1[:, 0, :]
    mean = jnp.sum(sums, axis=0, keepdims=True) / D
    apart = sums / F - mean
    var = (
        jnp.sum(stat1[:, 1, :], axis=0, keepdims=True)
        + F * jnp.sum(apart * apart, axis=0, keepdims=True)
    ) / D
    rstd = lax.rsqrt(var + 1e-06)
    normed = (xt - mean) * rstd
    normt[...] = normed
    chunk[...] = (normed * gaint[...]).astype(BF16)

    mine = pl.ds(pl.multiple_of(my_k * F, F), F)
    go(chunk, xb.at[r, pl.ds(pl.multiple_of((c % 4) * F, F), F)], sh_s, sh_r, owner)

    wbar = jnp.zeros((8, K), F32)
    for k in range(4):
        col = 4 * r + k
        cy, cx, ce = col // 8, (col // 2) % 4, col % 2
        gslot = (ce * 4 + (1 - ce) * cy + ce * cx) * 4 + (1 - ce) * cx + ce * cy
        grow = jnp.concatenate([stat1[gslot, 2:3, :], stat1[gslot, 3:4, 0:64]], axis=1)
        wbar += jnp.dot(split3(grow), w_ref[k * F:(k + 1) * F, :], preferred_element_type=F32)
    wz[r] = jnp.sum(wbar, axis=0, keepdims=True)

    ref = xb.at[my_q, mine]
    arrived(ref, sh_s, sh_r)
    for j in (1, 2, 3):
        go(ref, ref, xa_s.at[j - 1], xa_r.at[j - 1], apeer(j))
    for j in range(1, 8):
        go(wz.at[r], wz.at[r], wz_s.at[j - 1], wz_r.at[j - 1], zpeer(j))
    for j in (1, 2, 3):
        k = (my_k + 4 - j) % 4
        arrived(xb.at[my_q, pl.ds(pl.multiple_of(k * F, F), F)], xa_s.at[j - 1], xa_r.at[j - 1])
    ref = xb.at[my_q]
    for j in (1, 2, 3):
        go(ref, ref, xb_s.at[j - 1], xb_r.at[j - 1], bpeer(j))
    go(ref, ref, xc_s.at[0], xc_r.at[0], core)
    for j in (1, 3, 2):
        q = 2 * ((b + 3 + 4 - j) % 4) + e
        ref = xb.at[q]
        arrived(ref, xb_s.at[j - 1], xb_r.at[j - 1])
        go(ref, ref, xc_s.at[j], xc_r.at[j], core)
    for j in (0, 1, 3, 2):
        q = 2 * ((a + 3 + 4 - j) % 4) + 1 - e
        arrived(xb.at[q], xc_s.at[j], xc_r.at[j])

    def product(i, carry):
        odd = i % 2
        q = (r + (1 - odd) * (4 + i // 2) + odd * (3 - i // 2)) % 8
        part[q] = jnp.dot(xb[q].T, w_ref[...], preferred_element_type=F32)
        return carry

    def rs_slot(way, half, s):
        return (way * 2 + half) * 4 + s

    def rs_step(s):
        for half_of_plus in (0, 1):
            for way in (0, 1):
                half = half_of_plus if way == 0 else 1 - half_of_plus
                first = 0 if half_of_plus == 0 else 1
                if s < first:
                    continue
                cols = slice(half * HALF, (half + 1) * HALF)
                q = (r + 4 - s) % 8 if way == 0 else (r + 4 + s) % 8
                value = part[q, :, cols]
                n = rs_slot(way, half, s)
                if s > first:
                    arrived(rs_in.at[n - 1], rs_s.at[n - 1], rs_r.at[n - 1])
                    value = value + rs_in[n - 1].astype(F32)
                rs_out[n] = value.astype(BF16)
                to = zpeer(1) if way == 0 else zpeer(7)
                go(rs_out.at[n], rs_in.at[n], rs_s.at[n], rs_r.at[n], to)

    lax.fori_loop(0, 1, product, 0)
    rs_step(0)
    lax.fori_loop(1, 3, product, 0)
    rs_step(1)
    lax.fori_loop(3, 8, product, 0)
    rs_step(2)
    rs_step(3)
    for j in range(1, 8):
        arrived(wz.at[(r + 8 - j) % 8], wz_s.at[j - 1], wz_r.at[j - 1])
    wsum = split3(jnp.sum(wz[...], axis=0))
    for way in (0, 1):
        for half in (0, 1):
            n = rs_slot(way, half, 3)
            arrived(rs_in.at[n], rs_s.at[n], rs_r.at[n])

    def gelu(i, carry):
        rows = pl.ds(pl.multiple_of(i * 16, 16), 16)
        both = []
        for half in (0, 1):
            cols = slice(half * HALF, (half + 1) * HALF)
            both.append(
                part[r, rows, cols]
                + rs_in[rs_slot(0, half, 3), rows, :].astype(F32)
                + rs_in[rs_slot(1, half, 3), rows, :].astype(F32)
            )
        raw = jnp.concatenate(both, axis=1)
        v = raw + bias_ref[...]
        phi = 0.5 * (1.0 + lax.erf(v * SQRT_HALF))
        act_ref[rows, :] = (v * phi).astype(BF16)
        slope = phi + v * (INV_SQRT_2PI * jnp.exp(-0.5 * v * v))
        grad = (cot_ref[rows, :].astype(F32) * slope).astype(BF16)
        pg[r, rows, :] = grad
        pre[rows, :] = jnp.broadcast_to(
            jnp.sum(grad.astype(F32) * raw, axis=1, keepdims=True), (16, T)
        )
        return carry

    lax.fori_loop(0, 8, gelu, 0)

    def ag_send(t):
        for half_of_plus in (0, 1):
            for way in (0, 1):
                half = half_of_plus if way == 0 else 1 - half_of_plus
                if t == 4 and half_of_plus == 1:
                    continue
                q = (r + 8 - (t - 1)) % 8 if way == 0 else (r + t - 1) % 8
                n = (way * 2 + half) * 4 + t - 1
                ref = pg.at[q, :, pl.ds(half * HALF, HALF)]
                if t > 1:
                    arrived(ref, ag_s.at[n - 1], ag_r.at[n - 1])
                to = zpeer(1) if way == 0 else zpeer(7)
                go(ref, ref, ag_s.at[n], ag_r.at[n], to)

    def ag_rest(last):
        for way in (0, 1):
            half = way if last == 4 else 1 - way
            n = (way * 2 + half) * 4 + last - 1
            q = (r + 8 - last) % 8 if way == 0 else (r + last) % 8
            ref = pg.at[q, :, pl.ds(half * HALF, HALF)]
            arrived(ref, ag_s.at[n], ag_r.at[n])

    def back(q):
        return dot_nt(w_ref[...], pg[q])

    swap = (r + e) % 2
    conditional = []

    def pair(p, even, odd):
        q_mine = (r + 8 + (1 - swap) * even + swap * odd) % 8
        q_other = (r + 8 + (1 - swap) * odd + swap * even) % 8
        ce_out[p] = back(q_other).astype(BF16)
        go(ce_out.at[p], ce_in.at[p], ce_s.at[p], ce_r.at[p], core)
        value = back(q_mine)
        arrived(ce_in.at[p], ce_s.at[p], ce_r.at[p])
        value = value + ce_in[p].astype(F32)
        b_to = (q_mine // 2 + 1) % 4

        @pl.when(b_to == b)
        def _():
            own[...] = value

        @pl.when(b_to != b)
        def _():
            rb_out[p] = value.astype(BF16)
            send(rb_out.at[p], rb_in.at[b], rb_s.at[p], rb_r.at[b], place(r, a, b_to, e)).start()

        conditional.append((p, b_to))

    ag_send(1)
    second_col = pre[...].T[0:1, :]
    first = jnp.sum(dot_nt(wsum, pg[r]), axis=0, keepdims=True)
    stat2[slot] = jnp.zeros((8, T), F32)
    stat2[slot, 0:1, :] = first
    stat2[slot, 1:2, :] = second_col
    gather = plane_gather(stat2, s2_s, s2_r)
    next(gather)
    ag_send(2)
    next(gather)
    pair(0, 0, 1)
    ag_send(3)
    next(gather)
    pair(1, 2, -1)
    ag_send(4)
    next(gather)
    ag_rest(3)
    pair(2, -2, 3)
    ag_rest(4)
    pair(3, 4, -3)

    def weight(i, carry):
        rows = pl.ds(pl.multiple_of(i * 128, 128), 128)
        lhs = jnp.concatenate([xb[q, rows, :] for q in range(8)], axis=1)
        wg_ref[rows, :] = jnp.dot(lhs, pg[...].reshape(8 * T, K), preferred_element_type=F32)
        return carry

    lax.fori_loop(0, 6, weight, 0)
    ones = jnp.ones((16, 8 * T), BF16)
    bg_ref[...] = jnp.dot(ones, pg[...].reshape(8 * T, K), preferred_element_type=F32)[0:1, :]

    for j in (1, 2, 3):
        n = (b + j) % 4
        arrived(rb_in.at[n], rb_s.at[0], rb_r.at[n])
        own[...] += rb_in[n].astype(F32)
    for j in (1, 2, 3):
        k = (my_k + j) % 4
        ra_out[j - 1] = own[pl.ds(pl.multiple_of(k * F, F), F), :].astype(BF16)
        go(ra_out.at[j - 1], ra_in.at[j - 1], ra_s.at[j - 1], ra_r.at[j - 1], apeer(j))
    value = own[mine, :]
    for j in (1, 2, 3):
        arrived(ra_in.at[j - 1], ra_s.at[j - 1], ra_r.at[j - 1])
        value = value + ra_in[j - 1].astype(F32)
    home_out[...] = value.astype(BF16)
    go(home_out, home_in, hm_s, hm_r, home)
    arrived(home_in, hm_s, hm_r)

    grad = home_in[...].astype(F32)
    normed = normt[...]
    gz[r] = jnp.sum((grad * normed).T, axis=0, keepdims=True)
    for j in range(1, 8):
        go(gz.at[r], gz.at[r], gz_s.at[j - 1], gz_r.at[j - 1], zpeer(j))
    g = grad * gaint[...]
    first = jnp.sum(stat2[:, 0, :], axis=0, keepdims=True) / D
    second = jnp.sum(stat2[:, 1, :], axis=0, keepdims=True) / D
    xg_ref[...] = (rstd * (g - first - normed * second)).T.astype(BF16)
    for j in range(1, 8):
        arrived(gz.at[(r + 8 - j) % 8], gz_s.at[j - 1], gz_r.at[j - 1])
    gg_ref[...] = jnp.sum(gz[...], axis=0)

    for copy in pending:
        copy.wait_send()
    for p, b_to in conditional:
        @pl.when(b_to != b)
        def _():
            send(rb_out.at[p], rb_in.at[b], rb_s.at[p], rb_r.at[b], core).wait_send()


def body(tokens, norm_gain, up_weight, up_bias, cotangent):
    def vmem(shape, dtype):
        return pltpu.VMEM(shape, dtype)

    def sems(*shape):
        return pltpu.SemaphoreType.DMA(shape)

    scratch = [
        vmem((F, T), BF16), vmem((F, T), F32), vmem((F, T), F32),
        vmem((32, 8, T), F32), vmem((32, 8, T), F32),
        vmem((8, K, T), BF16), vmem((8, T, K), F32), vmem((T, T), F32), vmem((8, T, K), BF16),
        vmem((16, T, HALF), BF16), vmem((16, T, HALF), BF16),
        vmem((4, K, T), BF16), vmem((4, K, T), BF16),
        vmem((4, K, T), BF16), vmem((4, K, T), BF16), vmem((K, T), F32),
        vmem((3, F, T), BF16), vmem((3, F, T), BF16), vmem((F, T), BF16), vmem((F, T), BF16),
        vmem((8, 1, K), F32), vmem((8, 1, F), F32),
    ]
    scratch += [
        sems(7), sems(7), sems(7), sems(7), sems(), sems(), sems(3), sems(3), sems(3), sems(3),
        sems(4), sems(4), sems(7), sems(7), sems(7), sems(7), sems(16), sems(16), sems(16), sems(16),
        sems(4), sems(4), sems(4), sems(4), sems(3), sems(3), sems(), sems(),
    ]
    space = pl.BlockSpec(memory_space=pltpu.VMEM)
    act, xg, wg, bg, gg = pl.pallas_call(
        kernel,
        out_shape=[
            jax.ShapeDtypeStruct((T, K), BF16),
            jax.ShapeDtypeStruct((T, F), BF16),
            jax.ShapeDtypeStruct((K, K), F32),
            jax.ShapeDtypeStruct((1, K), F32),
            jax.ShapeDtypeStruct((1, F), F32),
        ],
        in_specs=[space] * 5,
        out_specs=[space] * 5,
        scratch_shapes=scratch,
        compiler_params=pltpu.CompilerParams(
            collective_id=0, has_side_effects=True, vmem_limit_bytes=48 * 2**20
        ),
        name="mlp_up",
    )(tokens, norm_gain.reshape(1, F), up_weight, up_bias.reshape(1, K), cotangent)
    return act, xg, wg, bg.reshape(K), gg.reshape(F)


def solution(mesh):
    in_specs = (P("row", "col"), P("col"), P("row", "col"), P("col"), P("row", "col"))
    out_specs = (P("row", "col"), P("row", "col"), P("row", "col"), P("col"), P("col"))
    return jax.shard_map(body, mesh=mesh, in_specs=in_specs, out_specs=out_specs, check_vma=False)
```

```python
import functools

import jax
import jax.numpy as jnp
from jax import lax
from jax.experimental import pallas as pl
from jax.experimental.pallas import tpu as pltpu
from jax.sharding import PartitionSpec as P

D = 6144
F = 192
T = 128
K = 768
HALF = K // 2
MESH = pl.DeviceIdType.MESH
F32 = jnp.float32
BF16 = jnp.bfloat16
SQRT_HALF = 0.7071067811865476
INV_SQRT_2PI = 0.3989422804014327


def split3(row):
    hi = row.astype(BF16).astype(F32)
    rest = row - hi
    mid = rest.astype(BF16).astype(F32)
    low = rest - mid
    at = lax.broadcasted_iota(jnp.int32, (8, row.shape[1]), 0)
    rows = jnp.where(at == 0, hi, jnp.where(at == 1, mid, jnp.where(at == 2, low, 0.0)))
    return rows.astype(BF16)


def dot_nt(a, b):
    return lax.dot_general(a, b, (((1,), (1,)), ((), ())), preferred_element_type=F32)


def kernel(
    tok_hbm, gain_hbm, w_hbm, bias_hbm, cot_hbm,
    act_ref, xg_ref, wg_ref, bg_ref, gg_ref,
    tok_ref, gain_ref, w_ref, bias_ref, cot_ref,
    normt, gaint, gaincol, stat1, stat2, zstat, xb, xn, part, pre, pg,
    rs_out, rs_in, ce_out, ce_in, rb_out, rb_in, own, ra_out, ra_in, home_out, home_in,
    wz, gz_out, gz,
    in_s, s1_s, s1_r, s2_s, s2_r, sh_s, sh_r, xa_s, xa_r, xb_s, xb_r, xc_s, xc_r, zs_s, zs_r,
    wz_s, wz_r, gz_s, gz_r, rs_s, rs_r, ag_s, ag_r, ce_s, ce_r, rb_s, rb_r, ra_s, ra_r, hm_s, hm_r,
):
    loads = [
        pltpu.make_async_copy(src, dst, in_s.at[i])
        for i, (src, dst) in enumerate([
            (tok_hbm, tok_ref), (gain_hbm, gain_ref), (w_hbm, w_ref), (bias_hbm, bias_ref), (cot_hbm, cot_ref),
        ])
    ]
    for load in loads:
        load.start()

    r = lax.axis_index("row")
    c = lax.axis_index("col")
    y = c // 8
    x = (c // 2) % 4
    e = c % 2
    a = (1 - e) * x + e * y
    b = (1 - e) * y + e * x

    def at(z, yy, xx, ee):
        return (z, (yy * 4 + xx) * 2 + ee)

    def place(z, aa, bb, ee):
        return at(z, (1 - ee) * bb + ee * aa, (1 - ee) * aa + ee * bb, ee)

    def zpeer(j):
        return at((r + j) % 8, y, x, e)

    def apeer(j):
        return place(r, (a + j) % 4, b, e)

    def bpeer(j):
        return place(r, a, (b + j) % 4, e)

    core = at(r, y, x, 1 - e)
    my_k = (a + 3) % 4
    my_q = 2 * ((b + 3) % 4) + e
    mine = pl.ds(pl.multiple_of(my_k * F, F), F)
    owner = place(c // 4, (c % 4 + 1) % 4, (r // 2 + 1) % 4, r % 2)
    home = (my_q, 4 * r + my_k)

    to_self = 4 * r + my_k == c

    def holder(j):
        return ((r + j) % 8, 4 * r + my_k)

    def summer(q):
        return place(c // 4, (c % 4 + 1) % 4, (q // 2 + 1) % 4, q % 2)

    peers = [zpeer(j) for j in range(1, 8)]
    peers += [apeer(j) for j in (1, 2, 3)] + [bpeer(j) for j in (1, 2, 3)]
    peers += [core, owner, home]
    peers += [holder(j) for j in range(1, 8)]
    sources = [q for q in range(8)]
    barrier = pltpu.get_barrier_semaphore()
    for peer in peers:
        pl.semaphore_signal(barrier, inc=1, device_id=peer, device_id_type=MESH)

    @pl.when(jnp.logical_not(to_self))
    def _():
        pl.semaphore_signal(barrier, inc=1, device_id=holder(0), device_id_type=MESH)

    for q in sources:
        @pl.when(jnp.logical_not(jnp.logical_and(to_self, my_q == q)))
        def _():
            pl.semaphore_signal(barrier, inc=1, device_id=summer(q), device_id_type=MESH)

    pl.semaphore_wait(barrier, len(peers) + 9 - 2 * to_self.astype(jnp.int32))

    def send(src, dst, ssem, rsem, to):
        return pltpu.make_async_remote_copy(
            src_ref=src, dst_ref=dst, send_sem=ssem, recv_sem=rsem, device_id=to, device_id_type=MESH
        )

    def arrived(dst, ssem, rsem):
        send(dst, dst, ssem, rsem, core).wait_recv()

    pending = []

    def go(src, dst, ssem, rsem, to):
        copy = send(src, dst, ssem, rsem, to)
        copy.start()
        pending.append(copy)

    def plane_gather(tiles, ssem, rsem):
        mine = (e * 4 + b) * 4
        for j in (1, 2, 3):
            ref = tiles.at[mine + a]
            go(ref, ref, ssem.at[j - 1], rsem.at[j - 1], apeer(j))
        yield
        for j in (1, 2, 3):
            arrived(tiles.at[mine + (a + 4 - j) % 4], ssem.at[j - 1], rsem.at[j - 1])
        for j in (1, 2, 3):
            ref = tiles.at[pl.ds(mine, 4)]
            go(ref, ref, ssem.at[j + 2], rsem.at[j + 2], bpeer(j))
        yield
        for j in (1, 2, 3):
            ref = tiles.at[pl.ds((e * 4 + (b + 4 - j) % 4) * 4, 4)]
            arrived(ref, ssem.at[j + 2], rsem.at[j + 2])
        ref = tiles.at[pl.ds(e * 16, 16)]
        go(ref, ref, ssem.at[6], rsem.at[6], core)
        yield
        arrived(tiles.at[pl.ds((1 - e) * 16, 16)], ssem.at[6], rsem.at[6])
        yield

    loads[0].wait()
    go(tok_ref, xb.at[r, pl.ds(pl.multiple_of((c % 4) * F, F), F)], sh_s, sh_r, owner)

    loads[1].wait()
    xt = tok_ref[...].astype(F32)
    total = jnp.sum(xt, axis=0, keepdims=True)
    dev = xt - total / F
    squares = jnp.sum(dev * dev, axis=0, keepdims=True)
    slot = (e * 4 + b) * 4 + a
    stat1[slot] = jnp.zeros((8, T), F32)
    stat1[slot, 0:1, :] = total
    stat1[slot, 1:2, :] = squares
    stat1[slot, 2:3, :] = gain_ref[:, 0:128]
    stat1[slot, 3:4, 0:64] = gain_ref[:, 128:192]
    gather = plane_gather(stat1, s1_s, s1_r)
    next(gather)

    def chunk(q, k):
        return xb.at[q, pl.ds(pl.multiple_of(k * F, F), F)]

    def spread(k, i):
        for j in (1, 3, 2):
            n = i * 3 + j - 1
            go(chunk(my_q, k), chunk(my_q, k), xb_s.at[n], xb_r.at[n], bpeer(j))

    ref = chunk(my_q, my_k)
    arrived(ref, sh_s, sh_r)
    for j in (1, 3, 2):
        go(ref, ref, xa_s.at[j - 1], xa_r.at[j - 1], apeer(j))
    spread(my_k, 0)
    next(gather)
    for j in (1, 3, 2):
        k = (my_k + 4 - j) % 4
        arrived(chunk(my_q, k), xa_s.at[j - 1], xa_r.at[j - 1])
        spread(k, j)
    go(xb.at[my_q], xb.at[my_q], xc_s.at[0], xc_r.at[0], core)
    next(gather)
    next(gather)
    sums = stat1[:, 0, :]
    mean = jnp.sum(sums, axis=0, keepdims=True) / D
    apart = sums / F - mean
    var = (
        jnp.sum(stat1[:, 1, :], axis=0, keepdims=True)
        + F * jnp.sum(apart * apart, axis=0, keepdims=True)
    ) / D
    rstd = lax.rsqrt(var + 1e-06)
    zstat[r] = jnp.zeros((8, T), F32)
    zstat[r, 0:1, :] = mean
    zstat[r, 1:2, :] = rstd
    for j in range(1, 8):
        go(zstat.at[r], zstat.at[r], zs_s.at[j - 1], zs_r.at[j - 1], zpeer(j))
    gaint[...] = jnp.broadcast_to(gain_ref[...], (T, F)).T
    normt[...] = (xt - mean) * rstd
    grows = []
    for k in range(4):
        col = 4 * r + k
        cy, cx, ce = col // 8, (col // 2) % 4, col % 2
        gslot = (ce * 4 + (1 - ce) * cy + ce * cx) * 4 + (1 - ce) * cx + ce * cy
        grow = jnp.concatenate([stat1[gslot, 2:3, :], stat1[gslot, 3:4, 0:64]], axis=1)
        gaincol[k * F:(k + 1) * F, :] = jnp.broadcast_to(grow, (T, F)).T
        grows.append(split3(grow))
    for j in (1, 3, 2):
        q = 2 * ((b + 3 + 4 - j) % 4) + e
        for i in range(4):
            k = (my_k + 4 - i) % 4
            n = i * 3 + j - 1
            arrived(chunk(q, k), xb_s.at[n], xb_r.at[n])
        go(xb.at[q], xb.at[q], xc_s.at[j], xc_r.at[j], core)
    for j in range(1, 8):
        arrived(zstat.at[(r + 8 - j) % 8], zs_s.at[j - 1], zs_r.at[j - 1])
    for j in (0, 1, 3, 2):
        q = 2 * ((a + 3 + 4 - j) % 4) + 1 - e
        arrived(xb.at[q], xc_s.at[j], xc_r.at[j])
    loads[2].wait()

    def product(i, carry):
        odd = i % 2
        q = (r + (1 - odd) * (4 + i // 2) + odd * (3 - i // 2)) % 8
        for k in range(4):
            rows = slice(k * F, (k + 1) * F)
            normed = (xb[q, rows, :].astype(F32) - zstat[q, 0:1, :]) * zstat[q, 1:2, :]
            xn[q, rows, :] = (normed * gaincol[rows, :]).astype(BF16)
        part[q] = jnp.dot(xn[q].T, w_ref[...], preferred_element_type=F32)
        return carry

    def rs_slot(way, half, s):
        return (way * 2 + half) * 4 + s

    def rs_step(s):
        for half_of_plus in (0, 1):
            for way in (0, 1):
                half = half_of_plus if way == 0 else 1 - half_of_plus
                first = 0 if half_of_plus == 0 else 1
                if s < first:
                    continue
                cols = slice(half * HALF, (half + 1) * HALF)
                q = (r + 4 - s) % 8 if way == 0 else (r + 4 + s) % 8
                value = part[q, :, cols]
                n = rs_slot(way, half, s)
                if s > first:
                    arrived(rs_in.at[n - 1], rs_s.at[n - 1], rs_r.at[n - 1])
                    value = value + rs_in[n - 1].astype(F32)
                rs_out[n] = value.astype(BF16)
                to = zpeer(1) if way == 0 else zpeer(7)
                go(rs_out.at[n], rs_in.at[n], rs_s.at[n], rs_r.at[n], to)

    lax.fori_loop(0, 1, product, 0)
    rs_step(0)
    lax.fori_loop(1, 3, product, 0)
    rs_step(1)
    lax.fori_loop(3, 8, product, 0)
    rs_step(2)
    wbar = jnp.zeros((8, K), F32)
    for k in range(4):
        wbar += jnp.dot(grows[k], w_ref[k * F:(k + 1) * F, :], preferred_element_type=F32)
    wz[r] = jnp.sum(wbar, axis=0, keepdims=True)
    for j in range(1, 8):
        go(wz.at[r], wz.at[r], wz_s.at[j - 1], wz_r.at[j - 1], zpeer(j))
    rs_step(3)
    loads[3].wait()
    loads[4].wait()
    for way in (0, 1):
        for half in (0, 1):
            n = rs_slot(way, half, 3)
            arrived(rs_in.at[n], rs_s.at[n], rs_r.at[n])

    for j in range(1, 8):
        arrived(wz.at[(r + 8 - j) % 8], wz_s.at[j - 1], wz_r.at[j - 1])
    wsum = split3(jnp.sum(wz[...], axis=0))

    bias = bias_ref[...].reshape(1, K)

    def gelu(i, carry):
        rows = pl.ds(pl.multiple_of(i * 16, 16), 16)
        both = []
        for half in (0, 1):
            cols = slice(half * HALF, (half + 1) * HALF)
            both.append(
                part[r, rows, cols]
                + rs_in[rs_slot(0, half, 3), rows, :].astype(F32)
                + rs_in[rs_slot(1, half, 3), rows, :].astype(F32)
            )
        raw = jnp.concatenate(both, axis=1)
        v = raw + bias
        phi = 0.5 * (1.0 + lax.erf(v * SQRT_HALF))
        act_ref[rows, :] = (v * phi).astype(BF16)
        slope = phi + v * (INV_SQRT_2PI * jnp.exp(-0.5 * v * v))
        grad = (cot_ref[rows, :].astype(F32) * slope).astype(BF16)
        pg[r, rows, :] = grad
        pre[rows, :] = jnp.broadcast_to(
            jnp.sum(grad.astype(F32) * raw, axis=1, keepdims=True), (16, T)
        )
        return carry

    lax.fori_loop(0, 8, gelu, 0)

    def ag_send(t):
        for half_of_plus in (0, 1):
            for way in (0, 1):
                half = half_of_plus if way == 0 else 1 - half_of_plus
                if t == 4 and half_of_plus == 1:
                    continue
                q = (r + 8 - (t - 1)) % 8 if way == 0 else (r + t - 1) % 8
                n = (way * 2 + half) * 4 + t - 1
                ref = pg.at[q, :, pl.ds(half * HALF, HALF)]
                if t > 1:
                    arrived(ref, ag_s.at[n - 1], ag_r.at[n - 1])
                to = zpeer(1) if way == 0 else zpeer(7)
                go(ref, ref, ag_s.at[n], ag_r.at[n], to)

    def ag_rest(last):
        for way in (0, 1):
            half = way if last == 4 else 1 - way
            n = (way * 2 + half) * 4 + last - 1
            q = (r + 8 - last) % 8 if way == 0 else (r + last) % 8
            ref = pg.at[q, :, pl.ds(half * HALF, HALF)]
            arrived(ref, ag_s.at[n], ag_r.at[n])

    def back(q):
        return dot_nt(w_ref[...], pg[q])

    swap = (r + e) % 2
    conditional = []

    def pair(p, even, odd):
        q_mine = (r + 8 + (1 - swap) * even + swap * odd) % 8
        q_other = (r + 8 + (1 - swap) * odd + swap * even) % 8
        ce_out[p] = back(q_other).astype(BF16)
        go(ce_out.at[p], ce_in.at[p], ce_s.at[p], ce_r.at[p], core)
        value = back(q_mine)
        arrived(ce_in.at[p], ce_s.at[p], ce_r.at[p])
        value = value + ce_in[p].astype(F32)
        b_to = (q_mine // 2 + 1) % 4

        @pl.when(b_to == b)
        def _():
            own[...] = value

        @pl.when(b_to != b)
        def _():
            rb_out[p] = value.astype(BF16)
            send(rb_out.at[p], rb_in.at[b], rb_s.at[p], rb_r.at[b], place(r, a, b_to, e)).start()

        conditional.append((p, b_to))

    ag_send(1)
    second_col = pre[...].T[0:1, :]
    first = jnp.sum(dot_nt(wsum, pg[r]), axis=0, keepdims=True)
    stat2[slot] = jnp.zeros((8, T), F32)
    stat2[slot, 0:1, :] = first
    stat2[slot, 1:2, :] = second_col
    gather = plane_gather(stat2, s2_s, s2_r)
    next(gather)
    ag_send(2)
    next(gather)
    pair(0, 0, 1)
    ag_send(3)
    next(gather)
    pair(1, 2, -1)
    ag_send(4)
    next(gather)
    ag_rest(3)
    pair(2, -2, 3)
    ag_rest(4)
    pair(3, 4, -3)

    def weight(i, carry):
        rows = pl.ds(pl.multiple_of(i * 128, 128), 128)
        lhs = jnp.concatenate([xn[q, rows, :] for q in range(8)], axis=1)
        wg_ref[rows, :] = jnp.dot(lhs, pg[...].reshape(8 * T, K), preferred_element_type=F32)
        return carry

    lax.fori_loop(0, 6, weight, 0)
    ones = jnp.ones((16, 8 * T), BF16)
    bg_ref[...] = jnp.dot(ones, pg[...].reshape(8 * T, K), preferred_element_type=F32)[0:1, :].reshape(K)

    for j in (1, 2, 3):
        n = (b + j) % 4
        arrived(rb_in.at[n], rb_s.at[0], rb_r.at[n])
        own[...] += rb_in[n].astype(F32)
    for j in (1, 2, 3):
        k = (my_k + j) % 4
        ra_out[j - 1] = own[pl.ds(pl.multiple_of(k * F, F), F), :].astype(BF16)
        go(ra_out.at[j - 1], ra_in.at[j - 1], ra_s.at[j - 1], ra_r.at[j - 1], apeer(j))
    value = own[mine, :]
    for j in (1, 2, 3):
        arrived(ra_in.at[j - 1], ra_s.at[j - 1], ra_r.at[j - 1])
        value = value + ra_in[j - 1].astype(F32)
    home_out[...] = value
    go(home_out, home_in, hm_s, hm_r, home)
    normed = (xb[my_q, mine, :].astype(F32) - zstat[my_q, 0:1, :]) * zstat[my_q, 1:2, :]
    row = jnp.sum((value * normed).T, axis=0, keepdims=True)
    gz_out[...] = jnp.zeros((8, T), F32)
    gz_out[0:1, :] = row[:, 0:128]
    gz_out[1:2, 0:64] = row[:, 128:192]
    for j in range(1, 8):
        go(gz_out, gz.at[my_q], gz_s.at[j], gz_r.at[my_q], holder(j))

    @pl.when(to_self)
    def _():
        gz[my_q] = gz_out[...]

    @pl.when(jnp.logical_not(to_self))
    def _():
        send(gz_out, gz.at[my_q], gz_s.at[0], gz_r.at[my_q], holder(0)).start()

    first = jnp.sum(stat2[:, 0, :], axis=0, keepdims=True) / D
    second = jnp.sum(stat2[:, 1, :], axis=0, keepdims=True) / D
    arrived(home_in, hm_s, hm_r)
    g = home_in[...] * gaint[...]
    xg_ref[...] = (rstd * (g - first - normt[...] * second)).astype(BF16)
    for q in sources:
        @pl.when(jnp.logical_not(jnp.logical_and(to_self, my_q == q)))
        def _():
            arrived(gz.at[q], gz_s.at[0], gz_r.at[q])

    row = jnp.sum(gz[...], axis=0)
    gg_ref[...] = jnp.concatenate([row[0:1, :], row[1:2, 0:64]], axis=1)

    @pl.when(jnp.logical_not(to_self))
    def _():
        send(gz_out, gz.at[my_q], gz_s.at[0], gz_r.at[my_q], holder(0)).wait_send()

    for copy in pending:
        copy.wait_send()
    for p, b_to in conditional:
        @pl.when(b_to != b)
        def _():
            send(rb_out.at[p], rb_in.at[b], rb_s.at[p], rb_r.at[b], core).wait_send()


def store(*refs):
    sem = refs[10]
    copies = [pltpu.make_async_copy(refs[i], refs[5 + i], sem.at[i]) for i in range(5)]
    for copy in copies:
        copy.start()
    for copy in copies:
        copy.wait()


def body(tokens, norm_gain, up_weight, up_bias, cotangent):
    def vmem(shape, dtype):
        return pltpu.VMEM(shape, dtype)

    def sems(*shape):
        return pltpu.SemaphoreType.DMA(shape)

    scratch = [
        vmem((F, T), BF16), vmem((1, F), F32), vmem((K, K), BF16), vmem((K,), F32), vmem((T, K), BF16),
        vmem((F, T), F32), vmem((F, T), F32), vmem((K, T), F32),
        vmem((32, 8, T), F32), vmem((32, 8, T), F32), vmem((8, 8, T), F32),
        vmem((8, K, T), BF16), vmem((8, K, T), BF16), vmem((8, T, K), F32), vmem((T, T), F32), vmem((8, T, K), BF16),
        vmem((16, T, HALF), BF16), vmem((16, T, HALF), BF16),
        vmem((4, K, T), BF16), vmem((4, K, T), BF16),
        vmem((4, K, T), BF16), vmem((4, K, T), BF16), vmem((K, T), F32),
        vmem((3, F, T), BF16), vmem((3, F, T), BF16), vmem((F, T), F32), vmem((F, T), F32),
        vmem((8, 1, K), F32), vmem((8, T), F32), vmem((8, 8, T), F32),
    ]
    scratch += [
        sems(5), sems(7), sems(7), sems(7), sems(7), sems(), sems(), sems(3), sems(3), sems(12), sems(12),
        sems(4), sems(4), sems(7), sems(7), sems(7), sems(7), sems(8), sems(8), sems(16), sems(16), sems(16), sems(16),
        sems(4), sems(4), sems(4), sems(4), sems(3), sems(3), sems(), sems(),
    ]
    space = pl.BlockSpec(memory_space=pltpu.VMEM)
    anywhere = pl.BlockSpec(memory_space=pl.ANY)
    shapes = [
        jax.ShapeDtypeStruct((T, K), BF16),
        jax.ShapeDtypeStruct((F, T), BF16),
        jax.ShapeDtypeStruct((K, K), F32),
        jax.ShapeDtypeStruct((K,), F32),
        jax.ShapeDtypeStruct((1, F), F32),
    ]
    results = pl.pallas_call(
        kernel,
        out_shape=shapes,
        in_specs=[pl.BlockSpec(memory_space=pltpu.HBM)] * 5,
        out_specs=[space] * 5,
        scratch_shapes=scratch,
        compiler_params=pltpu.CompilerParams(
            collective_id=0, has_side_effects=True, vmem_limit_bytes=48 * 2**20
        ),
        name="mlp_up",
    )(tokens.T, norm_gain.reshape(1, F), up_weight, up_bias, cotangent)
    act, xg, wg, bg, gg = pl.pallas_call(
        store,
        out_shape=shapes,
        in_specs=[space] * 5,
        out_specs=[anywhere] * 5,
        scratch_shapes=[sems(5)],
        name="store",
    )(*results)
    return act, xg.T, wg, bg, gg.reshape(F)


def solution(mesh):
    in_specs = (P("row", "col"), P("col"), P("row", "col"), P("col"), P("row", "col"))
    out_specs = (P("row", "col"), P("row", "col"), P("row", "col"), P("col"), P("col"))
    return jax.shard_map(body, mesh=mesh, in_specs=in_specs, out_specs=out_specs, check_vma=False)
```

```python
import functools

import jax
import jax.numpy as jnp
from jax import lax
from jax.experimental import pallas as pl
from jax.experimental.pallas import tpu as pltpu
from jax.sharding import PartitionSpec as P

D = 6144
F = 192
S = F // 4
T = 128
K = 768
G = 4
ROWS = T // G
MESH = pl.DeviceIdType.MESH
F32 = jnp.float32
BF16 = jnp.bfloat16
SQRT_HALF = 0.7071067811865476
INV_SQRT_2PI = 0.3989422804014327


def split3(row):
    hi = row.astype(BF16).astype(F32)
    rest = row - hi
    mid = rest.astype(BF16).astype(F32)
    low = rest - mid
    at = lax.broadcasted_iota(jnp.int32, (8, row.shape[1]), 0)
    rows = jnp.where(at == 0, hi, jnp.where(at == 1, mid, jnp.where(at == 2, low, 0.0)))
    return rows.astype(BF16)


def dot_nt(a, b):
    return lax.dot_general(a, b, (((1,), (1,)), ((), ())), preferred_element_type=F32)


def kernel(
    tok_hbm, gain_hbm, w_hbm, bias_hbm, cot_hbm,
    act_hbm, xg_hbm, wg_hbm, bg_hbm, gg_hbm,
    tok_ref, gain_ref, w_ref, bias_ref, cot_ref,
    normt, gaint, gaincol, stat1, stat2, zstat, xb, xn, part, pre, pg,
    rs_out, rs_in, ce_out, ce_in, ra_out, ra_in, rb_out, rb_in, home_out, home_in, dots, own,
    wz, gz_out, gz, act_ref, xg_ref, wg_ref, bg_ref, gg_ref,
    in_s, out_s, s1_s, s1_r, s2_s, s2_r, sh_s, sh_r, xa_s, xa_r, xb_s, xb_r, xc_s, xc_r, zs_s, zs_r,
    wz_s, wz_r, gz_s, gz_r, rs_s, rs_r, ag_s, ag_r, ce_s, ce_r, ra_s, ra_r, rb_s, rb_r, hm_s, hm_r,
):
    loads = [
        pltpu.make_async_copy(src, dst, in_s.at[i])
        for i, (src, dst) in enumerate([
            (tok_hbm, tok_ref), (gain_hbm, gain_ref), (w_hbm, w_ref), (bias_hbm, bias_ref), (cot_hbm, cot_ref),
        ])
    ]
    for load in loads:
        load.start()

    r = lax.axis_index("row")
    c = lax.axis_index("col")
    y = c // 8
    x = (c // 2) % 4
    e = c % 2
    a = (1 - e) * x + e * y
    b = (1 - e) * y + e * x

    def at(z, yy, xx, ee):
        return (z, (yy * 4 + xx) * 2 + ee)

    def place(z, aa, bb, ee):
        return at(z, (1 - ee) * bb + ee * aa, (1 - ee) * aa + ee * bb, ee)

    def zpeer(j):
        return at((r + j) % 8, y, x, e)

    def apeer(j):
        return place(r, (a + j) % 4, b, e)

    def bpeer(j):
        return place(r, a, (b + j) % 4, e)

    core = at(r, y, x, 1 - e)
    def turn(z):
        return (z // 2) % 2 + 2 * (1 - z % 2)

    def gatherer(k, bb, ee):
        z = c // 4
        return place(z, (k + 4 - turn(z)) % 4, bb, ee)

    my_k = (a + turn(r)) % 4
    my_q = 2 * b + e
    mine = pl.ds(pl.multiple_of(my_k * F, F), F)

    def holder(q):
        return (q, 4 * r + my_k)

    peers = [zpeer(j) for j in range(1, 8)]
    peers += [apeer(j) for j in (1, 2, 3)] + [bpeer(j) for j in (1, 2, 3)] + [core]
    peers += [holder(q) for q in range(8)]
    peers += [gatherer(c % 4, bb, ee) for bb in range(4) for ee in range(2)]
    barrier = pltpu.get_barrier_semaphore()
    for peer in peers:
        pl.semaphore_signal(barrier, inc=1, device_id=peer, device_id_type=MESH)

    pl.semaphore_wait(barrier, len(peers))

    def send(src, dst, ssem, rsem, to):
        return pltpu.make_async_remote_copy(
            src_ref=src, dst_ref=dst, send_sem=ssem, recv_sem=rsem, device_id=to, device_id_type=MESH
        )

    def arrived(dst, ssem, rsem):
        send(dst, dst, ssem, rsem, core).wait_recv()

    pending = []

    def go(src, dst, ssem, rsem, to):
        copy = send(src, dst, ssem, rsem, to)
        copy.start()
        pending.append(copy)

    def plane_gather(tiles, ssem, rsem):
        mine = (e * 4 + b) * 4
        for j in (1, 2, 3):
            ref = tiles.at[mine + a]
            go(ref, ref, ssem.at[j - 1], rsem.at[j - 1], apeer(j))
        yield
        for j in (1, 2, 3):
            arrived(tiles.at[mine + (a + 4 - j) % 4], ssem.at[j - 1], rsem.at[j - 1])
        for j in (1, 2, 3):
            ref = tiles.at[pl.ds(mine, 4)]
            go(ref, ref, ssem.at[j + 2], rsem.at[j + 2], bpeer(j))
        yield
        for j in (1, 2, 3):
            ref = tiles.at[pl.ds((e * 4 + (b + 4 - j) % 4) * 4, 4)]
            arrived(ref, ssem.at[j + 2], rsem.at[j + 2])
        ref = tiles.at[pl.ds(e * 16, 16)]
        go(ref, ref, ssem.at[6], rsem.at[6], core)
        yield
        arrived(tiles.at[pl.ds((1 - e) * 16, 16)], ssem.at[6], rsem.at[6])
        yield

    loads[0].wait()
    owner = gatherer(c % 4, r // 2, r % 2)
    go(tok_ref, xb.at[r, pl.ds(pl.multiple_of((c % 4) * F, F), F)], sh_s, sh_r, owner)

    loads[1].wait()
    xt = tok_ref[...].astype(F32)
    total = jnp.sum(xt, axis=0, keepdims=True)
    dev = xt - total / F
    squares = jnp.sum(dev * dev, axis=0, keepdims=True)
    slot = (e * 4 + b) * 4 + a
    stat1[slot] = jnp.zeros((8, T), F32)
    stat1[slot, 0:1, :] = total
    stat1[slot, 1:2, :] = squares
    stat1[slot, 2:3, :] = gain_ref[:, 0:128]
    stat1[slot, 3:4, 0:64] = gain_ref[:, 128:192]
    gather = plane_gather(stat1, s1_s, s1_r)
    next(gather)

    def chunk(q, k):
        return xb.at[q, pl.ds(pl.multiple_of(k * F, F), F)]

    def spread(k, i):
        for j in (1, 3, 2):
            n = i * 3 + j - 1
            go(chunk(my_q, k), chunk(my_q, k), xb_s.at[n], xb_r.at[n], bpeer(j))

    ref = chunk(my_q, my_k)
    arrived(ref, sh_s, sh_r)
    for j in (1, 3, 2):
        go(ref, ref, xa_s.at[j - 1], xa_r.at[j - 1], apeer(j))
    spread(my_k, 0)
    next(gather)
    for j in (1, 3, 2):
        k = (my_k + 4 - j) % 4
        arrived(chunk(my_q, k), xa_s.at[j - 1], xa_r.at[j - 1])
        spread(k, j)
    go(xb.at[my_q], xb.at[my_q], xc_s.at[0], xc_r.at[0], core)
    next(gather)
    next(gather)
    sums = stat1[:, 0, :]
    mean = jnp.sum(sums, axis=0, keepdims=True) / D
    apart = sums / F - mean
    var = (
        jnp.sum(stat1[:, 1, :], axis=0, keepdims=True)
        + F * jnp.sum(apart * apart, axis=0, keepdims=True)
    ) / D
    rstd = lax.rsqrt(var + 1e-06)
    zstat[r] = jnp.zeros((8, T), F32)
    zstat[r, 0:1, :] = mean
    zstat[r, 1:2, :] = rstd
    for j in range(1, 8):
        go(zstat.at[r], zstat.at[r], zs_s.at[j - 1], zs_r.at[j - 1], zpeer(j))
    for j in (1, 3, 2):
        q = 2 * ((b + 4 - j) % 4) + e
        for i in range(4):
            n = i * 3 + j - 1
            arrived(chunk(q, (my_k + 4 - i) % 4), xb_s.at[n], xb_r.at[n])
        go(xb.at[q], xb.at[q], xc_s.at[j], xc_r.at[j], core)
    grows = []
    for k in range(4):
        col = 4 * r + k
        cy, cx, ce = col // 8, (col // 2) % 4, col % 2
        gslot = (ce * 4 + (1 - ce) * cy + ce * cx) * 4 + (1 - ce) * cx + ce * cy
        grow = jnp.concatenate([stat1[gslot, 2:3, :], stat1[gslot, 3:4, 0:64]], axis=1)
        gaincol[k * F:(k + 1) * F, :] = jnp.broadcast_to(grow, (T, F)).T
        grows.append(split3(grow))
    loads[2].wait()
    for j in range(1, 8):
        arrived(zstat.at[(r + 8 - j) % 8], zs_s.at[j - 1], zs_r.at[j - 1])
    for j in (0, 1, 3, 2):
        q = 2 * ((a + 4 - j) % 4) + 1 - e
        arrived(xb.at[q], xc_s.at[j], xc_r.at[j])

    def product(i, carry):
        odd = i % 2
        q = (r + (1 - odd) * (4 + i // 2) + odd * (3 - i // 2)) % 8
        for k in range(4):
            rows = slice(k * F, (k + 1) * F)
            normed = (xb[q, rows, :].astype(F32) - zstat[q, 0:1, :]) * zstat[q, 1:2, :]
            xn[q, rows, :] = (normed * gaincol[rows, :]).astype(BF16)
        part[q] = jnp.dot(xn[q].T, w_ref[...], preferred_element_type=F32)
        return carry

    def slot_of(way, s, g):
        return (way * 4 + s) * G + g

    def rows_of(g):
        return pl.ds(g * ROWS, ROWS)

    def ahead(way):
        return zpeer(1) if way == 0 else zpeer(7)

    def rs_step(s, g, ways):
        for way in ways:
            first = 0 if way == g % 2 else 1
            if s < first:
                continue
            q = (r + 4 - s) % 8 if way == 0 else (r + 4 + s) % 8
            value = part[q, rows_of(g), :]
            n = slot_of(way, s, g)
            if s > first:
                m = slot_of(way, s - 1, g)
                arrived(rs_in.at[m], rs_s.at[m], rs_r.at[m])
                value = value + rs_in[m].astype(F32)
            rs_out[n] = value.astype(BF16)
            go(rs_out.at[n], rs_in.at[n], rs_s.at[n], rs_r.at[n], ahead(way))

    def ag_step(t, g):
        for way in (g % 2, 1 - g % 2):
            if t == 4 and way != g % 2:
                continue
            q = (r + 9 - t) % 8 if way == 0 else (r + t - 1) % 8
            ref = pg.at[q, rows_of(g)]
            n = slot_of(way, t - 1, g)
            if t > 1:
                m = slot_of(way, t - 2, g)
                arrived(ref, ag_s.at[m], ag_r.at[m])
            go(ref, ref, ag_s.at[n], ag_r.at[n], ahead(way))

    def ag_last(t, g):
        way = g % 2 if t == 4 else 1 - g % 2
        q = (r + 8 - t) % 8 if way == 0 else (r + t) % 8
        m = slot_of(way, t - 1, g)
        arrived(pg.at[q, rows_of(g)], ag_s.at[m], ag_r.at[m])

    lax.fori_loop(0, 1, product, 0)
    for g in range(G):
        rs_step(0, g, (g % 2,))
    lax.fori_loop(1, 3, product, 0)
    for g in range(G):
        rs_step(1, g, (1 - g % 2,))
    lax.fori_loop(3, 8, product, 0)
    for g in range(G):
        rs_step(1, g, (g % 2,))
    gaint[...] = jnp.broadcast_to(gain_ref[...], (T, F)).T
    normt[...] = (xt - mean) * rstd
    wbar = jnp.zeros((8, K), F32)
    for k in range(4):
        wbar += jnp.dot(grows[k], w_ref[k * F:(k + 1) * F, :], preferred_element_type=F32)
    wz[r] = jnp.sum(wbar, axis=0, keepdims=True)
    for j in range(1, 8):
        go(wz.at[r], wz.at[r], wz_s.at[j - 1], wz_r.at[j - 1], zpeer(j))
    for s in (2, 3):
        for g in range(G):
            rs_step(s, g, (g % 2, 1 - g % 2))
    loads[3].wait()
    loads[4].wait()
    bias = bias_ref[...].reshape(1, K)

    for g in range(G):
        rows = rows_of(g)
        raw = part[r, rows, :]
        for way in (g % 2, 1 - g % 2):
            m = slot_of(way, 3, g)
            arrived(rs_in.at[m], rs_s.at[m], rs_r.at[m])
            raw = raw + rs_in[m].astype(F32)
        v = raw + bias
        phi = 0.5 * (1.0 + lax.erf(v * SQRT_HALF))
        act_ref[rows, :] = (v * phi).astype(BF16)
        slope = phi + v * (INV_SQRT_2PI * jnp.exp(-0.5 * v * v))
        grad = (cot_ref[rows, :].astype(F32) * slope).astype(BF16)
        pg[r, rows, :] = grad
        ag_step(1, g)
        pre[rows, :] = jnp.broadcast_to(
            jnp.sum(grad.astype(F32) * raw, axis=1, keepdims=True), (ROWS, T)
        )
    stores = [
        pltpu.make_async_copy(src, dst, out_s.at[i])
        for i, (src, dst) in enumerate([
            (act_ref, act_hbm), (xg_ref, xg_hbm),
            (wg_ref.at[0:256], wg_hbm.at[0:256]), (wg_ref.at[256:512], wg_hbm.at[256:512]),
            (wg_ref.at[512:768], wg_hbm.at[512:768]), (bg_ref, bg_hbm), (gg_ref, gg_hbm),
        ])
    ]
    stores[0].start()
    for j in range(1, 8):
        arrived(wz.at[(r + 8 - j) % 8], wz_s.at[j - 1], wz_r.at[j - 1])
    wsum = split3(jnp.sum(wz[...], axis=0))

    swap = (r + e) % 2
    dots[...] = jnp.zeros((2 * T, T), F32)

    def pair(p, even, odd):
        q = (r + 8 + (1 - swap) * even + swap * odd) % 8
        q_other = (r + 8 + (1 - swap) * odd + swap * even) % 8
        both = dot_nt(w_ref[...], jnp.concatenate([pg[q_other], pg[q]], axis=0))
        ce_out[p] = both[:, :T].astype(BF16)
        go(ce_out.at[p], ce_in.at[p], ce_s.at[p], ce_r.at[p], core)
        own[p] = both[:, T:]
        yield
        arrived(ce_in.at[p], ce_s.at[p], ce_r.at[p])
        for j in (2, 1, 3):
            k = (my_k + j) % 4
            rows = pl.ds(pl.multiple_of(k * F, F), F)
            n = p * 3 + j - 1
            ra_out[n] = (own[p, rows, :] + ce_in[p, rows, :].astype(F32)).astype(BF16)
            go(ra_out.at[n], ra_in.at[n], ra_s.at[n], ra_r.at[n], apeer(j))
        value = own[p, mine, :] + ce_in[p, mine, :].astype(F32)
        yield
        for j in (1, 3, 2):
            n = p * 3 + j - 1
            arrived(ra_in.at[n], ra_s.at[n], ra_r.at[n])
            value = value + ra_in[n].astype(F32)
        own[p, 0:F, :] = value
        for j in (2, 1, 3):
            bb = (b + j) % 4
            n = p * 3 + j - 1
            rb_out[n] = own[p, pl.ds(pl.multiple_of(bb * S, S), S), :].astype(BF16)
            go(rb_out.at[n], rb_in.at[n], rb_s.at[n], rb_r.at[n], bpeer(j))
        yield
        at_b = pl.ds(pl.multiple_of(b * S, S), S)
        value = own[p, at_b, :]
        for j in (1, 3, 2):
            n = p * 3 + j - 1
            arrived(rb_in.at[n], rb_s.at[n], rb_r.at[n])
            value = value + rb_in[n].astype(F32)
        home_out[p] = value
        go(home_out.at[p], home_in.at[at_b], hm_s.at[p], hm_r.at[b], holder(q))
        raw = xb[q, pl.ds(pl.multiple_of(my_k * F + b * S, S), S), :].astype(F32)
        dots[at_b, :] += value * ((raw - zstat[q, 0:1, :]) * zstat[q, 1:2, :])
        yield

    def ag_all(t):
        for g in range(G):
            ag_step(t, g)

    second_col = pre[...].T[0:1, :]
    first = jnp.sum(dot_nt(wsum, pg[r]), axis=0, keepdims=True)
    stat2[slot] = jnp.zeros((8, T), F32)
    stat2[slot, 0:1, :] = first
    stat2[slot, 1:2, :] = second_col
    gather = plane_gather(stat2, s2_s, s2_r)
    next(gather)
    ag_all(2)
    next(gather)
    pairs = [pair(0, 0, 1), pair(1, 2, -1), pair(2, -2, 3), pair(3, 4, -3)]
    next(pairs[0])
    ag_all(3)
    next(gather)
    next(pairs[0])
    next(pairs[1])
    ag_all(4)
    next(gather)
    next(pairs[0])
    next(pairs[1])
    for g in range(G):
        ag_last(3, g)
    next(pairs[2])
    next(pairs[0])
    next(pairs[1])
    for g in range(G):
        ag_last(4, g)
    next(pairs[3])
    next(pairs[2])
    next(pairs[3])

    def weight(i):
        rows = slice(i * 256, (i + 1) * 256)
        lhs = jnp.concatenate([xn[q, rows, :] for q in range(8)], axis=1)
        wg_ref[rows, :] = jnp.dot(lhs, pg[...].reshape(8 * T, K), preferred_element_type=F32)
        stores[2 + i].start()

    weight(0)
    next(pairs[1])
    weight(1)
    next(pairs[2])
    next(pairs[3])
    weight(2)
    ones = jnp.ones((16, 8 * T), BF16)
    bg_ref[...] = jnp.dot(ones, pg[...].reshape(8 * T, K), preferred_element_type=F32)[0:1, :].reshape(K)
    stores[5].start()
    next(pairs[2])
    next(pairs[3])

    for half in (0, 1):
        gz_out[half:half + 1, :] = jnp.sum(dots[half * T:(half + 1) * T, :].T, axis=0, keepdims=True)
    gz_out[2:8, :] = jnp.zeros((6, T), F32)
    for q in range(8):
        go(gz_out, gz.at[e * 4 + b], gz_s.at[q], gz_r.at[e * 4 + b], holder(q))

    first = jnp.sum(stat2[:, 0, :], axis=0, keepdims=True) / D
    second = jnp.sum(stat2[:, 1, :], axis=0, keepdims=True) / D
    for n in range(4):
        arrived(home_in.at[n * S:(n + 1) * S], hm_s.at[0], hm_r.at[n])
    g = home_in[...] * gaint[...]
    xg_ref[...] = (rstd * (g - first - normt[...] * second)).astype(BF16)
    stores[1].start()
    for n in range(8):
        arrived(gz.at[n], gz_s.at[0], gz_r.at[n])
    row = jnp.sum(gz[...], axis=0)
    gg_ref[...] = jnp.concatenate([row[0:1, :], row[1:2, 0:64]], axis=1)
    stores[6].start()

    for copy in stores:
        copy.wait()
    for copy in pending:
        copy.wait_send()

def store(*refs):
    ins, outs, held = refs[:5], refs[5:10], refs[10:15]
    in_sem, out_sem = refs[15:]
    rows = K // 8
    parts = [(ins[i], held[i], outs[i]) for i in (0, 1, 3, 4)]
    for i in range(8):
        at = pl.ds(i * rows, rows)
        parts.append((ins[2].at[at], held[2].at[at], outs[2].at[at]))
    loads = [pltpu.make_async_copy(src, mid, in_sem.at[i]) for i, (src, mid, _) in enumerate(parts)]
    stores = [pltpu.make_async_copy(mid, dst, out_sem.at[i]) for i, (_, mid, dst) in enumerate(parts)]
    for load in loads:
        load.start()
    for load, copy in zip(loads, stores):
        load.wait()
        copy.start()
    for copy in stores:
        copy.wait()


def body(tokens, norm_gain, up_weight, up_bias, cotangent):
    def vmem(shape, dtype):
        return pltpu.VMEM(shape, dtype)

    def sems(*shape):
        return pltpu.SemaphoreType.DMA(shape)

    scratch = [
        vmem((F, T), BF16), vmem((1, F), F32), vmem((K, K), BF16), vmem((K,), F32), vmem((T, K), BF16),
        vmem((F, T), F32), vmem((F, T), F32), vmem((K, T), F32),
        vmem((32, 8, T), F32), vmem((32, 8, T), F32), vmem((8, 8, T), F32),
        vmem((8, K, T), BF16), vmem((8, K, T), BF16), vmem((8, T, K), F32), vmem((T, T), F32), vmem((8, T, K), BF16),
        vmem((8 * G, ROWS, K), BF16), vmem((8 * G, ROWS, K), BF16),
        vmem((4, K, T), BF16), vmem((4, K, T), BF16),
        vmem((12, F, T), BF16), vmem((12, F, T), BF16), vmem((12, S, T), BF16), vmem((12, S, T), BF16),
        vmem((4, S, T), F32), vmem((F, T), F32), vmem((2 * T, T), F32), vmem((4, K, T), F32),
        vmem((8, 1, K), F32), vmem((8, T), F32), vmem((8, 8, T), F32),
        vmem((T, K), BF16), vmem((F, T), BF16), vmem((K, K), F32), vmem((K,), F32), vmem((1, F), F32),
    ]
    scratch += [
        sems(5), sems(7), sems(7), sems(7), sems(7), sems(7), sems(), sems(), sems(3), sems(3), sems(12), sems(12),
        sems(4), sems(4), sems(7), sems(7), sems(7), sems(7), sems(8), sems(8),
        sems(8 * G), sems(8 * G), sems(8 * G), sems(8 * G),
        sems(4), sems(4), sems(12), sems(12), sems(12), sems(12), sems(4), sems(4),
    ]
    anywhere = pl.BlockSpec(memory_space=pl.ANY)
    shapes = [
        jax.ShapeDtypeStruct((T, K), BF16),
        jax.ShapeDtypeStruct((F, T), BF16),
        jax.ShapeDtypeStruct((K, K), F32),
        jax.ShapeDtypeStruct((K,), F32),
        jax.ShapeDtypeStruct((1, F), F32),
    ]
    results = pl.pallas_call(
        kernel,
        out_shape=shapes,
        in_specs=[pl.BlockSpec(memory_space=pltpu.HBM)] * 5,
        out_specs=[anywhere] * 5,
        scratch_shapes=scratch,
        compiler_params=pltpu.CompilerParams(
            collective_id=0, has_side_effects=True, vmem_limit_bytes=58 * 2**20
        ),
        name="mlp_up",
    )(tokens.T, norm_gain.reshape(1, F), up_weight, up_bias, cotangent)
    act, xg, wg, bg, gg = pl.pallas_call(
        store,
        out_shape=shapes,
        in_specs=[anywhere] * 5,
        out_specs=[anywhere] * 5,
        scratch_shapes=[vmem(t.shape, t.dtype) for t in shapes] + [sems(12), sems(12)],
        compiler_params=pltpu.CompilerParams(vmem_limit_bytes=60 * 2**20),
        name="store",
    )(*results)
    return act, xg.T, wg, bg, gg.reshape(F)


def solution(mesh):
    in_specs = (P("row", "col"), P("col"), P("row", "col"), P("col"), P("row", "col"))
    out_specs = (P("row", "col"), P("row", "col"), P("row", "col"), P("col"), P("col"))
    return jax.shard_map(body, mesh=mesh, in_specs=in_specs, out_specs=out_specs, check_vma=False)
```

```python
import functools

import jax
import jax.numpy as jnp
from jax import lax
from jax.experimental import pallas as pl
from jax.experimental.pallas import tpu as pltpu
from jax.sharding import PartitionSpec as P

D = 6144
F = 192
T = 128
K = 768
G = 4
ROWS = T // G
MESH = pl.DeviceIdType.MESH
F32 = jnp.float32
BF16 = jnp.bfloat16
SQRT_HALF = 0.7071067811865476
INV_SQRT_2PI = 0.3989422804014327


def split3(row):
    hi = row.astype(BF16).astype(F32)
    rest = row - hi
    mid = rest.astype(BF16).astype(F32)
    low = rest - mid
    at = lax.broadcasted_iota(jnp.int32, (8, row.shape[1]), 0)
    rows = jnp.where(at == 0, hi, jnp.where(at == 1, mid, jnp.where(at == 2, low, 0.0)))
    return rows.astype(BF16)


def dot_nt(a, b):
    return lax.dot_general(a, b, (((1,), (1,)), ((), ())), preferred_element_type=F32)


def kernel(
    tok_hbm, gain_hbm, w_hbm, bias_hbm, cot_hbm,
    act_hbm, xg_hbm, wg_hbm, bg_hbm, gg_hbm,
    tok_ref, gain_ref, w_ref, bias_ref, cot_ref,
    normt, gaint, gaincol, stat1, stat2, zstat, xb, xn, part, pre, pg,
    rs_out, rs_in, ce_out, ce_in, ra_out, ra_in, home_out, home_in, dots, own,
    wz, gz_out, gz, act_ref, xg_ref, wg_ref, bg_ref, gg_ref,
    in_s, out_s, s1_s, s1_r, s2_s, s2_r, sh_s, sh_r, xa_s, xa_r, xb_s, xb_r, xc_s, xc_r, zs_s, zs_r,
    wz_s, wz_r, gz_s, gz_r, rs_s, rs_r, ag_s, ag_r, ce_s, ce_r, ra_s, ra_r, hm_s, hm_r,
):
    loads = [
        pltpu.make_async_copy(src, dst, in_s.at[i])
        for i, (src, dst) in enumerate([
            (tok_hbm, tok_ref), (gain_hbm, gain_ref), (w_hbm, w_ref), (bias_hbm, bias_ref), (cot_hbm, cot_ref),
        ])
    ]
    for load in loads:
        load.start()

    r = lax.axis_index("row")
    c = lax.axis_index("col")
    y = c // 8
    x = (c // 2) % 4
    e = c % 2
    a = (1 - e) * x + e * y
    b = (1 - e) * y + e * x

    def at(z, yy, xx, ee):
        return (z, (yy * 4 + xx) * 2 + ee)

    def place(z, aa, bb, ee):
        return at(z, (1 - ee) * bb + ee * aa, (1 - ee) * aa + ee * bb, ee)

    def zpeer(j):
        return at((r + j) % 8, y, x, e)

    def apeer(j):
        return place(r, (a + j) % 4, b, e)

    def bpeer(j):
        return place(r, a, (b + j) % 4, e)

    core = at(r, y, x, 1 - e)
    def turn(z):
        return (z // 2) % 2 + 2 * (1 - z % 2)

    def gatherer(k, bb, ee):
        z = c // 4
        return place(z, (k + 4 - turn(z)) % 4, bb, ee)

    my_k = (a + turn(r)) % 4
    my_q = 2 * b + e
    mine = pl.ds(pl.multiple_of(my_k * F, F), F)

    def holder(q):
        return (q, 4 * r + my_k)

    peers = [zpeer(j) for j in range(1, 8)]
    peers += [apeer(j) for j in (1, 2, 3)] + [bpeer(j) for j in (1, 2, 3)] + [core]
    peers += [holder(q) for q in range(8)]
    peers += [gatherer(c % 4, bb, ee) for bb in range(4) for ee in range(2)]
    barrier = pltpu.get_barrier_semaphore()
    for peer in peers:
        pl.semaphore_signal(barrier, inc=1, device_id=peer, device_id_type=MESH)

    pl.semaphore_wait(barrier, len(peers))

    def send(src, dst, ssem, rsem, to):
        return pltpu.make_async_remote_copy(
            src_ref=src, dst_ref=dst, send_sem=ssem, recv_sem=rsem, device_id=to, device_id_type=MESH
        )

    def arrived(dst, ssem, rsem):
        send(dst, dst, ssem, rsem, core).wait_recv()

    pending = []

    def go(src, dst, ssem, rsem, to):
        copy = send(src, dst, ssem, rsem, to)
        copy.start()
        pending.append(copy)

    def plane_gather(tiles, ssem, rsem):
        mine = (e * 4 + b) * 4
        for j in (1, 2, 3):
            ref = tiles.at[mine + a]
            go(ref, ref, ssem.at[j - 1], rsem.at[j - 1], apeer(j))
        yield
        for j in (1, 2, 3):
            arrived(tiles.at[mine + (a + 4 - j) % 4], ssem.at[j - 1], rsem.at[j - 1])
        for j in (1, 2, 3):
            ref = tiles.at[pl.ds(mine, 4)]
            go(ref, ref, ssem.at[j + 2], rsem.at[j + 2], bpeer(j))
        yield
        for j in (1, 2, 3):
            ref = tiles.at[pl.ds((e * 4 + (b + 4 - j) % 4) * 4, 4)]
            arrived(ref, ssem.at[j + 2], rsem.at[j + 2])
        ref = tiles.at[pl.ds(e * 16, 16)]
        go(ref, ref, ssem.at[6], rsem.at[6], core)
        yield
        arrived(tiles.at[pl.ds((1 - e) * 16, 16)], ssem.at[6], rsem.at[6])
        yield

    loads[0].wait()
    owner = gatherer(c % 4, r // 2, r % 2)
    go(tok_ref, xb.at[r, pl.ds(pl.multiple_of((c % 4) * F, F), F)], sh_s, sh_r, owner)

    loads[1].wait()
    xt = tok_ref[...].astype(F32)
    total = jnp.sum(xt, axis=0, keepdims=True)
    dev = xt - total / F
    squares = jnp.sum(dev * dev, axis=0, keepdims=True)
    slot = (e * 4 + b) * 4 + a
    stat1[slot] = jnp.zeros((8, T), F32)
    stat1[slot, 0:1, :] = total
    stat1[slot, 1:2, :] = squares
    stat1[slot, 2:3, :] = gain_ref[:, 0:128]
    stat1[slot, 3:4, 0:64] = gain_ref[:, 128:192]
    gather = plane_gather(stat1, s1_s, s1_r)
    next(gather)

    def chunk(q, k):
        return xb.at[q, pl.ds(pl.multiple_of(k * F, F), F)]

    def spread(k, i):
        for j in (2, 1, 3):
            n = i * 3 + j - 1
            go(chunk(my_q, k), chunk(my_q, k), xb_s.at[n], xb_r.at[n], bpeer(j))

    next(gather)
    ref = chunk(my_q, my_k)
    arrived(ref, sh_s, sh_r)
    for j in (2, 1, 3):
        go(ref, ref, xa_s.at[j - 1], xa_r.at[j - 1], apeer(j))
    spread(my_k, 0)
    next(gather)
    next(gather)
    sums = stat1[:, 0, :]
    mean = jnp.sum(sums, axis=0, keepdims=True) / D
    apart = sums / F - mean
    var = (
        jnp.sum(stat1[:, 1, :], axis=0, keepdims=True)
        + F * jnp.sum(apart * apart, axis=0, keepdims=True)
    ) / D
    rstd = lax.rsqrt(var + 1e-06)
    zstat[r] = jnp.zeros((8, T), F32)
    zstat[r, 0:1, :] = mean
    zstat[r, 1:2, :] = rstd
    for j in range(1, 8):
        go(zstat.at[r], zstat.at[r], zs_s.at[j - 1], zs_r.at[j - 1], zpeer(j))
    for j in (1, 3, 2):
        k = (my_k + 4 - j) % 4
        arrived(chunk(my_q, k), xa_s.at[j - 1], xa_r.at[j - 1])
        spread(k, j)
    go(xb.at[my_q], xb.at[my_q], xc_s.at[0], xc_r.at[0], core)
    for j in (1, 3, 2):
        q = 2 * ((b + 4 - j) % 4) + e
        for i in range(4):
            n = i * 3 + j - 1
            arrived(chunk(q, (my_k + 4 - i) % 4), xb_s.at[n], xb_r.at[n])
        go(xb.at[q], xb.at[q], xc_s.at[j], xc_r.at[j], core)
    grows = []
    for k in range(4):
        col = 4 * r + k
        cy, cx, ce = col // 8, (col // 2) % 4, col % 2
        gslot = (ce * 4 + (1 - ce) * cy + ce * cx) * 4 + (1 - ce) * cx + ce * cy
        grow = jnp.concatenate([stat1[gslot, 2:3, :], stat1[gslot, 3:4, 0:64]], axis=1)
        gaincol[k * F:(k + 1) * F, :] = jnp.broadcast_to(grow, (T, F)).T
        grows.append(split3(grow))
    loads[2].wait()
    for j in range(1, 8):
        arrived(zstat.at[(r + 8 - j) % 8], zs_s.at[j - 1], zs_r.at[j - 1])
    for j in (0, 1, 3, 2):
        q = 2 * ((a + 4 - j) % 4) + 1 - e
        arrived(xb.at[q], xc_s.at[j], xc_r.at[j])

    def product(i, carry):
        odd = i % 2
        q = (r + (1 - odd) * (4 + i // 2) + odd * (3 - i // 2)) % 8
        for k in range(4):
            rows = slice(k * F, (k + 1) * F)
            normed = (xb[q, rows, :].astype(F32) - zstat[q, 0:1, :]) * zstat[q, 1:2, :]
            xn[q, rows, :] = (normed * gaincol[rows, :]).astype(BF16)
        part[q] = jnp.dot(xn[q].T, w_ref[...], preferred_element_type=F32)
        return carry

    def slot_of(way, s, g):
        return (way * 4 + s) * G + g

    def rows_of(g):
        return pl.ds(g * ROWS, ROWS)

    def ahead(way):
        return zpeer(1) if way == 0 else zpeer(7)

    def rs_step(s, g, ways):
        for way in ways:
            first = 0 if way == g % 2 else 1
            if s < first:
                continue
            q = (r + 4 - s) % 8 if way == 0 else (r + 4 + s) % 8
            value = part[q, rows_of(g), :]
            n = slot_of(way, s, g)
            if s > first:
                m = slot_of(way, s - 1, g)
                arrived(rs_in.at[m], rs_s.at[m], rs_r.at[m])
                value = value + rs_in[m].astype(F32)
            rs_out[n] = value.astype(BF16)
            go(rs_out.at[n], rs_in.at[n], rs_s.at[n], rs_r.at[n], ahead(way))

    def ag_step(t, g):
        for way in (g % 2, 1 - g % 2):
            if t == 4 and way != g % 2:
                continue
            q = (r + 9 - t) % 8 if way == 0 else (r + t - 1) % 8
            ref = pg.at[q, rows_of(g)]
            n = slot_of(way, t - 1, g)
            if t > 1:
                m = slot_of(way, t - 2, g)
                arrived(ref, ag_s.at[m], ag_r.at[m])
            go(ref, ref, ag_s.at[n], ag_r.at[n], ahead(way))

    def ag_last(t, g):
        way = g % 2 if t == 4 else 1 - g % 2
        q = (r + 8 - t) % 8 if way == 0 else (r + t) % 8
        m = slot_of(way, t - 1, g)
        arrived(pg.at[q, rows_of(g)], ag_s.at[m], ag_r.at[m])

    lax.fori_loop(0, 1, product, 0)
    for g in range(G):
        rs_step(0, g, (g % 2,))
    lax.fori_loop(1, 3, product, 0)
    for g in range(G):
        rs_step(1, g, (1 - g % 2,))
    lax.fori_loop(3, 8, product, 0)
    for g in range(G):
        rs_step(1, g, (g % 2,))
    gaint[...] = jnp.broadcast_to(gain_ref[...], (T, F)).T
    normt[...] = (xt - mean) * rstd
    wbar = jnp.zeros((8, K), F32)
    for k in range(4):
        wbar += jnp.dot(grows[k], w_ref[k * F:(k + 1) * F, :], preferred_element_type=F32)
    wz[r] = jnp.sum(wbar, axis=0, keepdims=True)
    for j in range(1, 8):
        go(wz.at[r], wz.at[r], wz_s.at[j - 1], wz_r.at[j - 1], zpeer(j))
    for s in (2, 3):
        for g in range(G):
            rs_step(s, g, (g % 2, 1 - g % 2))
    loads[3].wait()
    loads[4].wait()
    bias = bias_ref[...].reshape(1, K)

    for g in range(G):
        rows = rows_of(g)
        raw = part[r, rows, :]
        for way in (g % 2, 1 - g % 2):
            m = slot_of(way, 3, g)
            arrived(rs_in.at[m], rs_s.at[m], rs_r.at[m])
            raw = raw + rs_in[m].astype(F32)
        v = raw + bias
        phi = 0.5 * (1.0 + lax.erf(v * SQRT_HALF))
        act_ref[rows, :] = (v * phi).astype(BF16)
        slope = phi + v * (INV_SQRT_2PI * jnp.exp(-0.5 * v * v))
        grad = (cot_ref[rows, :].astype(F32) * slope).astype(BF16)
        pg[r, rows, :] = grad
        ag_step(1, g)
        pre[rows, :] = jnp.broadcast_to(
            jnp.sum(grad.astype(F32) * raw, axis=1, keepdims=True), (ROWS, T)
        )
    stores = [
        pltpu.make_async_copy(src, dst, out_s.at[i])
        for i, (src, dst) in enumerate([
            (act_ref, act_hbm), (xg_ref, xg_hbm),
            (wg_ref.at[0:256], wg_hbm.at[0:256]), (wg_ref.at[256:512], wg_hbm.at[256:512]),
            (wg_ref.at[512:768], wg_hbm.at[512:768]), (bg_ref, bg_hbm), (gg_ref, gg_hbm),
        ])
    ]
    stores[0].start()
    for j in range(1, 8):
        arrived(wz.at[(r + 8 - j) % 8], wz_s.at[j - 1], wz_r.at[j - 1])
    wsum = split3(jnp.sum(wz[...], axis=0))

    swap = (r + e) % 2
    dots[...] = jnp.zeros((F, T), F32)

    def pair(p, even, odd):
        q = (r + 8 + (1 - swap) * even + swap * odd) % 8
        q_other = (r + 8 + (1 - swap) * odd + swap * even) % 8
        both = dot_nt(w_ref[...], jnp.concatenate([pg[q_other], pg[q]], axis=0))
        ce_out[p] = both[:, :T].astype(BF16)
        go(ce_out.at[p], ce_in.at[p], ce_s.at[p], ce_r.at[p], core)
        own[p] = both[:, T:]
        yield
        arrived(ce_in.at[p], ce_s.at[p], ce_r.at[p])
        for j in (2, 1, 3):
            k = (my_k + j) % 4
            rows = pl.ds(pl.multiple_of(k * F, F), F)
            n = p * 3 + j - 1
            ra_out[n] = (own[p, rows, :] + ce_in[p, rows, :].astype(F32)).astype(BF16)
            go(ra_out.at[n], ra_in.at[n], ra_s.at[n], ra_r.at[n], apeer(j))
        value = own[p, mine, :] + ce_in[p, mine, :].astype(F32)
        yield
        for j in (1, 3, 2):
            n = p * 3 + j - 1
            arrived(ra_in.at[n], ra_s.at[n], ra_r.at[n])
            value = value + ra_in[n].astype(F32)
        home_out[p] = value.astype(BF16)
        go(home_out.at[p], home_in.at[b], hm_s.at[p], hm_r.at[b], holder(q))
        raw = xb[q, mine, :].astype(F32)
        dots[...] += value * ((raw - zstat[q, 0:1, :]) * zstat[q, 1:2, :])
        yield

    def ag_all(t):
        for g in range(G):
            ag_step(t, g)

    second_col = pre[...].T[0:1, :]
    first = jnp.sum(dot_nt(wsum, pg[r]), axis=0, keepdims=True)
    stat2[slot] = jnp.zeros((8, T), F32)
    stat2[slot, 0:1, :] = first
    stat2[slot, 1:2, :] = second_col
    gather = plane_gather(stat2, s2_s, s2_r)
    next(gather)
    ag_all(2)
    next(gather)
    pairs = [pair(0, 0, 1), pair(1, 2, -1), pair(2, -2, 3), pair(3, 4, -3)]
    next(pairs[0])
    ag_all(3)
    next(gather)
    next(pairs[0])
    next(pairs[1])
    ag_all(4)
    next(gather)
    next(pairs[0])
    next(pairs[1])
    for g in range(G):
        ag_last(3, g)
    next(pairs[2])
    next(pairs[1])
    for g in range(G):
        ag_last(4, g)
    next(pairs[3])
    next(pairs[2])
    next(pairs[3])

    def weight(i):
        rows = slice(i * 256, (i + 1) * 256)
        lhs = jnp.concatenate([xn[q, rows, :] for q in range(8)], axis=1)
        wg_ref[rows, :] = jnp.dot(lhs, pg[...].reshape(8 * T, K), preferred_element_type=F32)
        stores[2 + i].start()

    weight(0)
    next(pairs[2])
    next(pairs[3])
    row = jnp.sum(dots[...].T, axis=0, keepdims=True)
    gz_out[0:1, :] = row[:, 0:128]
    gz_out[1:2, :] = jnp.concatenate([row[:, 128:192], jnp.zeros((1, 64), F32)], axis=1)
    gz_out[2:8, :] = jnp.zeros((6, T), F32)
    for q in range(8):
        go(gz_out, gz.at[e * 4 + b], gz_s.at[q], gz_r.at[e * 4 + b], holder(q))

    weight(1)
    weight(2)
    ones = jnp.ones((16, 8 * T), BF16)
    bg_ref[...] = jnp.dot(ones, pg[...].reshape(8 * T, K), preferred_element_type=F32)[0:1, :].reshape(K)
    stores[5].start()

    first = jnp.sum(stat2[:, 0, :], axis=0, keepdims=True) / D
    second = jnp.sum(stat2[:, 1, :], axis=0, keepdims=True) / D
    total = jnp.zeros((F, T), F32)
    for n in range(4):
        arrived(home_in.at[n], hm_s.at[0], hm_r.at[n])
        total = total + home_in[n].astype(F32)
    g = total * gaint[...]
    xg_ref[...] = (rstd * (g - first - normt[...] * second)).astype(BF16)
    stores[1].start()
    for n in range(8):
        arrived(gz.at[n], gz_s.at[0], gz_r.at[n])
    row = jnp.sum(gz[...], axis=0)
    gg_ref[...] = jnp.concatenate([row[0:1, :], row[1:2, 0:64]], axis=1)
    stores[6].start()

    for copy in stores:
        copy.wait()
    for copy in pending:
        copy.wait_send()

def store(*refs):
    ins, outs, held = refs[:5], refs[5:10], refs[10:15]
    in_sem, out_sem = refs[15:]
    rows = K // 8
    parts = [(ins[i], held[i], outs[i]) for i in (0, 1, 3, 4)]
    for i in range(8):
        at = pl.ds(i * rows, rows)
        parts.append((ins[2].at[at], held[2].at[at], outs[2].at[at]))
    loads = [pltpu.make_async_copy(src, mid, in_sem.at[i]) for i, (src, mid, _) in enumerate(parts)]
    stores = [pltpu.make_async_copy(mid, dst, out_sem.at[i]) for i, (_, mid, dst) in enumerate(parts)]
    for load in loads:
        load.start()
    for load, copy in zip(loads, stores):
        load.wait()
        copy.start()
    for copy in stores:
        copy.wait()


def body(tokens, norm_gain, up_weight, up_bias, cotangent):
    def vmem(shape, dtype):
        return pltpu.VMEM(shape, dtype)

    def sems(*shape):
        return pltpu.SemaphoreType.DMA(shape)

    scratch = [
        vmem((F, T), BF16), vmem((1, F), F32), vmem((K, K), BF16), vmem((K,), F32), vmem((T, K), BF16),
        vmem((F, T), F32), vmem((F, T), F32), vmem((K, T), F32),
        vmem((32, 8, T), F32), vmem((32, 8, T), F32), vmem((8, 8, T), F32),
        vmem((8, K, T), BF16), vmem((8, K, T), BF16), vmem((8, T, K), F32), vmem((T, T), F32), vmem((8, T, K), BF16),
        vmem((8 * G, ROWS, K), BF16), vmem((8 * G, ROWS, K), BF16),
        vmem((4, K, T), BF16), vmem((4, K, T), BF16),
        vmem((12, F, T), BF16), vmem((12, F, T), BF16),
        vmem((4, F, T), BF16), vmem((4, F, T), BF16), vmem((F, T), F32), vmem((4, K, T), F32),
        vmem((8, 1, K), F32), vmem((8, T), F32), vmem((8, 8, T), F32),
        vmem((T, K), BF16), vmem((F, T), BF16), vmem((K, K), F32), vmem((K,), F32), vmem((1, F), F32),
    ]
    scratch += [
        sems(5), sems(7), sems(7), sems(7), sems(7), sems(7), sems(), sems(), sems(3), sems(3), sems(12), sems(12),
        sems(4), sems(4), sems(7), sems(7), sems(7), sems(7), sems(8), sems(8),
        sems(8 * G), sems(8 * G), sems(8 * G), sems(8 * G),
        sems(4), sems(4), sems(12), sems(12), sems(4), sems(4),
    ]
    anywhere = pl.BlockSpec(memory_space=pl.ANY)
    shapes = [
        jax.ShapeDtypeStruct((T, K), BF16),
        jax.ShapeDtypeStruct((F, T), BF16),
        jax.ShapeDtypeStruct((K, K), F32),
        jax.ShapeDtypeStruct((K,), F32),
        jax.ShapeDtypeStruct((1, F), F32),
    ]
    results = pl.pallas_call(
        kernel,
        out_shape=shapes,
        in_specs=[pl.BlockSpec(memory_space=pltpu.HBM)] * 5,
        out_specs=[anywhere] * 5,
        scratch_shapes=scratch,
        compiler_params=pltpu.CompilerParams(
            collective_id=0, has_side_effects=True, vmem_limit_bytes=58 * 2**20
        ),
        name="mlp_up",
    )(tokens.T, norm_gain.reshape(1, F), up_weight, up_bias, cotangent)
    act, xg, wg, bg, gg = pl.pallas_call(
        store,
        out_shape=shapes,
        in_specs=[anywhere] * 5,
        out_specs=[anywhere] * 5,
        scratch_shapes=[vmem(t.shape, t.dtype) for t in shapes] + [sems(12), sems(12)],
        compiler_params=pltpu.CompilerParams(vmem_limit_bytes=60 * 2**20),
        name="store",
    )(*results)
    return act, xg.T, wg, bg, gg.reshape(F)


def solution(mesh):
    in_specs = (P("row", "col"), P("col"), P("row", "col"), P("col"), P("row", "col"))
    out_specs = (P("row", "col"), P("row", "col"), P("row", "col"), P("col"), P("col"))
    return jax.shard_map(body, mesh=mesh, in_specs=in_specs, out_specs=out_specs, check_vma=False)
```

```python
import functools

import jax
import jax.numpy as jnp
from jax import lax
from jax.experimental import pallas as pl
from jax.experimental.pallas import tpu as pltpu
from jax.sharding import PartitionSpec as P

D = 6144
F = 192
T = 128
K = 768
G = 4
ROWS = T // G
MESH = pl.DeviceIdType.MESH
F32 = jnp.float32
BF16 = jnp.bfloat16
SQRT_HALF = 0.7071067811865476
INV_SQRT_2PI = 0.3989422804014327


def split3(row):
    hi = row.astype(BF16).astype(F32)
    rest = row - hi
    mid = rest.astype(BF16).astype(F32)
    low = rest - mid
    at = lax.broadcasted_iota(jnp.int32, (8, row.shape[1]), 0)
    rows = jnp.where(at == 0, hi, jnp.where(at == 1, mid, jnp.where(at == 2, low, 0.0)))
    return rows.astype(BF16)


def dot_nt(a, b):
    return lax.dot_general(a, b, (((1,), (1,)), ((), ())), preferred_element_type=F32)


def kernel(
    tok_hbm, gain_hbm, w_hbm, bias_hbm, cot_hbm,
    act_hbm, xg_hbm, wg_hbm, bg_hbm, gg_hbm,
    tok_ref, gain_ref, w_ref, bias_ref, cot_ref,
    normt, gaint, gaincol, stat1, stat2, zstat, xb, xn, part, pre, pg,
    rs_out, rs_in, ce_out, ce_in, ra_out, ra_in, home_out, home_in, dots, own,
    wz, gz_out, gz, act_ref, xg_ref, wg_ref, bg_ref, gg_ref,
    in_s, out_s, s1_s, s1_r, s2_s, s2_r, sh_s, sh_r, xa_s, xa_r, xb_s, xb_r, xc_s, xc_r, zs_s, zs_r,
    wz_s, wz_r, gz_s, gz_r, rs_s, rs_r, ag_s, ag_r, ce_s, ce_r, ra_s, ra_r, hm_s, hm_r,
):
    loads = [
        pltpu.make_async_copy(src, dst, in_s.at[i])
        for i, (src, dst) in enumerate([
            (tok_hbm, tok_ref), (gain_hbm, gain_ref), (w_hbm, w_ref), (bias_hbm, bias_ref), (cot_hbm, cot_ref),
        ])
    ]
    for load in loads:
        load.start()

    r = lax.axis_index("row")
    c = lax.axis_index("col")
    y = c // 8
    x = (c // 2) % 4
    e = c % 2
    a = (1 - e) * x + e * y
    b = (1 - e) * y + e * x

    def at(z, yy, xx, ee):
        return (z, (yy * 4 + xx) * 2 + ee)

    def place(z, aa, bb, ee):
        return at(z, (1 - ee) * bb + ee * aa, (1 - ee) * aa + ee * bb, ee)

    def zpeer(j):
        return at((r + j) % 8, y, x, e)

    def apeer(j):
        return place(r, (a + j) % 4, b, e)

    def bpeer(j):
        return place(r, a, (b + j) % 4, e)

    core = at(r, y, x, 1 - e)
    def turn(z):
        return (z // 2) % 2 + 2 * (1 - z % 2)

    def gatherer(k, bb, ee):
        z = c // 4
        return place(z, (k + 4 - turn(z)) % 4, bb, ee)

    my_k = (a + turn(r)) % 4
    my_q = 2 * b + e
    mine = pl.ds(pl.multiple_of(my_k * F, F), F)

    def holder(q):
        return (q, 4 * r + my_k)

    peers = [zpeer(j) for j in range(1, 8)]
    peers += [apeer(j) for j in (1, 2, 3)] + [bpeer(j) for j in (1, 2, 3)] + [core]
    peers += [holder(q) for q in range(8)]
    peers += [gatherer(c % 4, bb, ee) for bb in range(4) for ee in range(2)]
    barrier = pltpu.get_barrier_semaphore()
    for peer in peers:
        pl.semaphore_signal(barrier, inc=1, device_id=peer, device_id_type=MESH)

    pl.semaphore_wait(barrier, len(peers))

    def send(src, dst, ssem, rsem, to):
        return pltpu.make_async_remote_copy(
            src_ref=src, dst_ref=dst, send_sem=ssem, recv_sem=rsem, device_id=to, device_id_type=MESH
        )

    def arrived(dst, ssem, rsem):
        send(dst, dst, ssem, rsem, core).wait_recv()

    pending = []

    def go(src, dst, ssem, rsem, to):
        copy = send(src, dst, ssem, rsem, to)
        copy.start()
        pending.append(copy)

    def plane_gather(tiles, ssem, rsem):
        mine = (e * 4 + b) * 4
        for j in (1, 2, 3):
            ref = tiles.at[mine + a]
            go(ref, ref, ssem.at[j - 1], rsem.at[j - 1], apeer(j))
        yield
        for j in (1, 2, 3):
            arrived(tiles.at[mine + (a + 4 - j) % 4], ssem.at[j - 1], rsem.at[j - 1])
        for j in (1, 2, 3):
            ref = tiles.at[pl.ds(mine, 4)]
            go(ref, ref, ssem.at[j + 2], rsem.at[j + 2], bpeer(j))
        yield
        for j in (1, 2, 3):
            ref = tiles.at[pl.ds((e * 4 + (b + 4 - j) % 4) * 4, 4)]
            arrived(ref, ssem.at[j + 2], rsem.at[j + 2])
        ref = tiles.at[pl.ds(e * 16, 16)]
        go(ref, ref, ssem.at[6], rsem.at[6], core)
        yield
        arrived(tiles.at[pl.ds((1 - e) * 16, 16)], ssem.at[6], rsem.at[6])
        yield

    loads[0].wait()
    owner = gatherer(c % 4, r // 2, r % 2)
    go(tok_ref, xb.at[r, pl.ds(pl.multiple_of((c % 4) * F, F), F)], sh_s, sh_r, owner)

    loads[1].wait()
    xt = tok_ref[...].astype(F32)
    total = jnp.sum(xt, axis=0, keepdims=True)
    dev = xt - total / F
    squares = jnp.sum(dev * dev, axis=0, keepdims=True)
    slot = (e * 4 + b) * 4 + a
    stat1[slot] = jnp.zeros((8, T), F32)
    stat1[slot, 0:1, :] = total
    stat1[slot, 1:2, :] = squares
    stat1[slot, 2:3, :] = gain_ref[:, 0:128]
    stat1[slot, 3:4, 0:64] = gain_ref[:, 128:192]
    gather = plane_gather(stat1, s1_s, s1_r)
    next(gather)

    def chunk(q, k):
        return xb.at[q, pl.ds(pl.multiple_of(k * F, F), F)]

    def spread(k, i):
        for j in (2, 1, 3):
            n = i * 3 + j - 1
            go(chunk(my_q, k), chunk(my_q, k), xb_s.at[n], xb_r.at[n], bpeer(j))

    next(gather)
    ref = chunk(my_q, my_k)
    arrived(ref, sh_s, sh_r)
    for j in (2, 1, 3):
        go(ref, ref, xa_s.at[j - 1], xa_r.at[j - 1], apeer(j))
    spread(my_k, 0)
    next(gather)
    next(gather)
    sums = stat1[:, 0, :]
    mean = jnp.sum(sums, axis=0, keepdims=True) / D
    apart = sums / F - mean
    var = (
        jnp.sum(stat1[:, 1, :], axis=0, keepdims=True)
        + F * jnp.sum(apart * apart, axis=0, keepdims=True)
    ) / D
    rstd = lax.rsqrt(var + 1e-06)
    zstat[r] = jnp.zeros((8, T), F32)
    zstat[r, 0:1, :] = mean
    zstat[r, 1:2, :] = rstd
    for j in range(1, 8):
        go(zstat.at[r], zstat.at[r], zs_s.at[j - 1], zs_r.at[j - 1], zpeer(j))
    for j in (1, 3, 2):
        k = (my_k + 4 - j) % 4
        arrived(chunk(my_q, k), xa_s.at[j - 1], xa_r.at[j - 1])
        spread(k, j)
    go(xb.at[my_q], xb.at[my_q], xc_s.at[0], xc_r.at[0], core)
    for j in (1, 3, 2):
        q = 2 * ((b + 4 - j) % 4) + e
        for i in range(4):
            n = i * 3 + j - 1
            arrived(chunk(q, (my_k + 4 - i) % 4), xb_s.at[n], xb_r.at[n])
        go(xb.at[q], xb.at[q], xc_s.at[j], xc_r.at[j], core)
    grows = []
    for k in range(4):
        col = 4 * r + k
        cy, cx, ce = col // 8, (col // 2) % 4, col % 2
        gslot = (ce * 4 + (1 - ce) * cy + ce * cx) * 4 + (1 - ce) * cx + ce * cy
        grow = jnp.concatenate([stat1[gslot, 2:3, :], stat1[gslot, 3:4, 0:64]], axis=1)
        gaincol[k * F:(k + 1) * F, :] = jnp.broadcast_to(grow, (T, F)).T
        grows.append(split3(grow))
    loads[2].wait()
    for j in range(1, 8):
        arrived(zstat.at[(r + 8 - j) % 8], zs_s.at[j - 1], zs_r.at[j - 1])
    for j in (0, 1, 3, 2):
        q = 2 * ((a + 4 - j) % 4) + 1 - e
        arrived(xb.at[q], xc_s.at[j], xc_r.at[j])

    def product(i, carry):
        odd = i % 2
        q = (r + (1 - odd) * (4 + i // 2) + odd * (3 - i // 2)) % 8
        for k in range(4):
            rows = slice(k * F, (k + 1) * F)
            normed = (xb[q, rows, :].astype(F32) - zstat[q, 0:1, :]) * zstat[q, 1:2, :]
            xn[q, rows, :] = (normed * gaincol[rows, :]).astype(BF16)
        part[q] = jnp.dot(xn[q].T, w_ref[...], preferred_element_type=F32)
        return carry

    def slot_of(way, s, g):
        return (way * 4 + s) * G + g

    def rows_of(g):
        return pl.ds(g * ROWS, ROWS)

    def ahead(way):
        return zpeer(1) if way == 0 else zpeer(7)

    def rs_step(s, g, ways):
        for way in ways:
            first = 0 if way == g % 2 else 1
            if s < first:
                continue
            q = (r + 4 - s) % 8 if way == 0 else (r + 4 + s) % 8
            value = part[q, rows_of(g), :]
            n = slot_of(way, s, g)
            if s > first:
                m = slot_of(way, s - 1, g)
                arrived(rs_in.at[m], rs_s.at[m], rs_r.at[m])
                value = value + rs_in[m].astype(F32)
            rs_out[n] = value.astype(BF16)
            go(rs_out.at[n], rs_in.at[n], rs_s.at[n], rs_r.at[n], ahead(way))

    def ag_step(t, g):
        for way in (g % 2, 1 - g % 2):
            if t == 4 and way != g % 2:
                continue
            q = (r + 9 - t) % 8 if way == 0 else (r + t - 1) % 8
            ref = pg.at[q, rows_of(g)]
            n = slot_of(way, t - 1, g)
            if t > 1:
                m = slot_of(way, t - 2, g)
                arrived(ref, ag_s.at[m], ag_r.at[m])
            go(ref, ref, ag_s.at[n], ag_r.at[n], ahead(way))

    def ag_last(t, g):
        way = g % 2 if t == 4 else 1 - g % 2
        q = (r + 8 - t) % 8 if way == 0 else (r + t) % 8
        m = slot_of(way, t - 1, g)
        arrived(pg.at[q, rows_of(g)], ag_s.at[m], ag_r.at[m])

    lax.fori_loop(0, 1, product, 0)
    for g in range(G):
        rs_step(0, g, (g % 2,))
    lax.fori_loop(1, 3, product, 0)
    for g in range(G):
        rs_step(1, g, (1 - g % 2,))
    lax.fori_loop(3, 8, product, 0)
    for g in range(G):
        rs_step(1, g, (g % 2,))
    gaint[...] = jnp.broadcast_to(gain_ref[...], (T, F)).T
    normt[...] = (xt - mean) * rstd
    wbar = jnp.zeros((8, K), F32)
    for k in range(4):
        wbar += jnp.dot(grows[k], w_ref[k * F:(k + 1) * F, :], preferred_element_type=F32)
    wz[r] = jnp.sum(wbar, axis=0, keepdims=True)
    for j in range(1, 8):
        go(wz.at[r], wz.at[r], wz_s.at[j - 1], wz_r.at[j - 1], zpeer(j))
    for s in (2, 3):
        for g in range(G):
            rs_step(s, g, (g % 2, 1 - g % 2))
    loads[3].wait()
    loads[4].wait()
    bias = bias_ref[...].reshape(1, K)

    for g in range(G):
        rows = rows_of(g)
        raw = part[r, rows, :]
        for way in (g % 2, 1 - g % 2):
            m = slot_of(way, 3, g)
            arrived(rs_in.at[m], rs_s.at[m], rs_r.at[m])
            raw = raw + rs_in[m].astype(F32)
        v = raw + bias
        phi = 0.5 * (1.0 + lax.erf(v * SQRT_HALF))
        act_ref[rows, :] = (v * phi).astype(BF16)
        slope = phi + v * (INV_SQRT_2PI * jnp.exp(-0.5 * v * v))
        grad = (cot_ref[rows, :].astype(F32) * slope).astype(BF16)
        pg[r, rows, :] = grad
        ag_step(1, g)
        pre[rows, :] = jnp.broadcast_to(
            jnp.sum(grad.astype(F32) * raw, axis=1, keepdims=True), (ROWS, T)
        )
    stores = [
        pltpu.make_async_copy(src, dst, out_s.at[i])
        for i, (src, dst) in enumerate([
            (act_ref, act_hbm), (xg_ref, xg_hbm),
            (wg_ref.at[0:256], wg_hbm.at[0:256]), (wg_ref.at[256:512], wg_hbm.at[256:512]),
            (wg_ref.at[512:768], wg_hbm.at[512:768]), (bg_ref, bg_hbm), (gg_ref, gg_hbm),
        ])
    ]
    stores[0].start()
    for j in range(1, 8):
        arrived(wz.at[(r + 8 - j) % 8], wz_s.at[j - 1], wz_r.at[j - 1])
    wsum = split3(jnp.sum(wz[...], axis=0))

    swap = (r + e) % 2
    dots[...] = jnp.zeros((F, T), F32)

    def pair(p, even, odd):
        q = (r + 8 + (1 - swap) * even + swap * odd) % 8
        q_other = (r + 8 + (1 - swap) * odd + swap * even) % 8
        both = dot_nt(w_ref[...], jnp.concatenate([pg[q_other], pg[q]], axis=0))
        ce_out[p] = both[:, :T].astype(BF16)
        go(ce_out.at[p], ce_in.at[p], ce_s.at[p], ce_r.at[p], core)
        own[p] = both[:, T:]
        yield
        arrived(ce_in.at[p], ce_s.at[p], ce_r.at[p])
        for j in (2, 1, 3):
            k = (my_k + j) % 4
            rows = pl.ds(pl.multiple_of(k * F, F), F)
            n = p * 3 + j - 1
            ra_out[n] = (own[p, rows, :] + ce_in[p, rows, :].astype(F32)).astype(BF16)
            go(ra_out.at[n], ra_in.at[n], ra_s.at[n], ra_r.at[n], apeer(j))
        value = own[p, mine, :] + ce_in[p, mine, :].astype(F32)
        yield
        for j in (1, 3, 2):
            n = p * 3 + j - 1
            arrived(ra_in.at[n], ra_s.at[n], ra_r.at[n])
            value = value + ra_in[n].astype(F32)
        home_out[p] = value.astype(BF16)
        go(home_out.at[p], home_in.at[b], hm_s.at[p], hm_r.at[b], holder(q))
        raw = xb[q, mine, :].astype(F32)
        dots[...] += value * ((raw - zstat[q, 0:1, :]) * zstat[q, 1:2, :])
        yield

    def ag_all(t):
        for g in range(G):
            ag_step(t, g)

    second_col = pre[...].T[0:1, :]
    first = jnp.sum(dot_nt(wsum, pg[r]), axis=0, keepdims=True)
    stat2[slot] = jnp.zeros((8, T), F32)
    stat2[slot, 0:1, :] = first
    stat2[slot, 1:2, :] = second_col
    gather = plane_gather(stat2, s2_s, s2_r)
    next(gather)
    ag_all(2)
    next(gather)
    pairs = [pair(0, 0, 1), pair(1, 2, -1), pair(2, -2, 3), pair(3, 4, -3)]
    next(pairs[0])
    ag_all(3)
    next(gather)
    next(pairs[0])
    next(pairs[1])
    ag_all(4)
    next(gather)
    next(pairs[0])
    next(pairs[1])
    for g in range(G):
        ag_last(3, g)
    next(pairs[2])
    next(pairs[1])
    for g in range(G):
        ag_last(4, g)
    next(pairs[3])
    next(pairs[2])
    next(pairs[3])

    def weight(i):
        rows = slice(i * 256, (i + 1) * 256)
        lhs = jnp.concatenate([xn[q, rows, :] for q in range(8)], axis=1)
        wg_ref[rows, :] = jnp.dot(lhs, pg[...].reshape(8 * T, K), preferred_element_type=F32)
        stores[2 + i].start()

    weight(0)
    next(pairs[2])
    next(pairs[3])
    row = jnp.sum(dots[...].T, axis=0, keepdims=True)
    gz_out[0:1, :] = row[:, 0:128]
    gz_out[1:2, :] = jnp.concatenate([row[:, 128:192], jnp.zeros((1, 64), F32)], axis=1)
    for q in range(8):
        go(gz_out.at[0:2], gz.at[e * 4 + b, 0:2], gz_s.at[q], gz_r.at[e * 4 + b], holder(q))

    weight(1)
    weight(2)
    for copy in pending[:-13]:
        copy.wait_send()
    del pending[:-13]
    ones = jnp.ones((16, 8 * T), BF16)
    bg_ref[...] = jnp.dot(ones, pg[...].reshape(8 * T, K), preferred_element_type=F32)[0:1, :].reshape(K)
    stores[5].start()

    first = jnp.sum(stat2[:, 0, :], axis=0, keepdims=True) / D
    second = jnp.sum(stat2[:, 1, :], axis=0, keepdims=True) / D
    total = jnp.zeros((F, T), F32)
    for n in range(4):
        arrived(home_in.at[n], hm_s.at[0], hm_r.at[n])
        total = total + home_in[n].astype(F32)
    g = total * gaint[...]
    xg_ref[...] = (rstd * (g - first - normt[...] * second)).astype(BF16)
    stores[1].start()
    for n in range(8):
        arrived(gz.at[n, 0:2], gz_s.at[0], gz_r.at[n])
    row = jnp.sum(gz[:, 0:2, :], axis=0)
    gg_ref[...] = jnp.concatenate([row[0:1, :], row[1:2, 0:64]], axis=1)
    stores[6].start()

    for copy in stores:
        copy.wait()
    for copy in pending:
        copy.wait_send()

def store(*refs):
    ins, outs, held = refs[:5], refs[5:10], refs[10:15]
    in_sem, out_sem = refs[15:]
    rows = K // 8
    parts = [(ins[i], held[i], outs[i]) for i in (0, 1, 3, 4)]
    for i in range(8):
        at = pl.ds(i * rows, rows)
        parts.append((ins[2].at[at], held[2].at[at], outs[2].at[at]))
    loads = [pltpu.make_async_copy(src, mid, in_sem.at[i]) for i, (src, mid, _) in enumerate(parts)]
    stores = [pltpu.make_async_copy(mid, dst, out_sem.at[i]) for i, (_, mid, dst) in enumerate(parts)]
    for load in loads:
        load.start()
    for load, copy in zip(loads, stores):
        load.wait()
        copy.start()
    for copy in stores:
        copy.wait()


def body(tokens, norm_gain, up_weight, up_bias, cotangent):
    def vmem(shape, dtype):
        return pltpu.VMEM(shape, dtype)

    def sems(*shape):
        return pltpu.SemaphoreType.DMA(shape)

    scratch = [
        vmem((F, T), BF16), vmem((1, F), F32), vmem((K, K), BF16), vmem((K,), F32), vmem((T, K), BF16),
        vmem((F, T), F32), vmem((F, T), F32), vmem((K, T), F32),
        vmem((32, 8, T), F32), vmem((32, 8, T), F32), vmem((8, 8, T), F32),
        vmem((8, K, T), BF16), vmem((8, K, T), BF16), vmem((8, T, K), F32), vmem((T, T), F32), vmem((8, T, K), BF16),
        vmem((8 * G, ROWS, K), BF16), vmem((8 * G, ROWS, K), BF16),
        vmem((4, K, T), BF16), vmem((4, K, T), BF16),
        vmem((12, F, T), BF16), vmem((12, F, T), BF16),
        vmem((4, F, T), BF16), vmem((4, F, T), BF16), vmem((F, T), F32), vmem((4, K, T), F32),
        vmem((8, 1, K), F32), vmem((8, T), F32), vmem((8, 8, T), F32),
        vmem((T, K), BF16), vmem((F, T), BF16), vmem((K, K), F32), vmem((K,), F32), vmem((1, F), F32),
    ]
    scratch += [
        sems(5), sems(7), sems(7), sems(7), sems(7), sems(7), sems(), sems(), sems(3), sems(3), sems(12), sems(12),
        sems(4), sems(4), sems(7), sems(7), sems(7), sems(7), sems(8), sems(8),
        sems(8 * G), sems(8 * G), sems(8 * G), sems(8 * G),
        sems(4), sems(4), sems(12), sems(12), sems(4), sems(4),
    ]
    anywhere = pl.BlockSpec(memory_space=pl.ANY)
    shapes = [
        jax.ShapeDtypeStruct((T, K), BF16),
        jax.ShapeDtypeStruct((F, T), BF16),
        jax.ShapeDtypeStruct((K, K), F32),
        jax.ShapeDtypeStruct((K,), F32),
        jax.ShapeDtypeStruct((1, F), F32),
    ]
    results = pl.pallas_call(
        kernel,
        out_shape=shapes,
        in_specs=[pl.BlockSpec(memory_space=pltpu.HBM)] * 5,
        out_specs=[anywhere] * 5,
        scratch_shapes=scratch,
        compiler_params=pltpu.CompilerParams(
            collective_id=0, has_side_effects=True, vmem_limit_bytes=58 * 2**20
        ),
        name="mlp_up",
    )(tokens.T, norm_gain.reshape(1, F), up_weight, up_bias, cotangent)
    act, xg, wg, bg, gg = pl.pallas_call(
        store,
        out_shape=shapes,
        in_specs=[anywhere] * 5,
        out_specs=[anywhere] * 5,
        scratch_shapes=[vmem(t.shape, t.dtype) for t in shapes] + [sems(12), sems(12)],
        compiler_params=pltpu.CompilerParams(vmem_limit_bytes=60 * 2**20),
        name="store",
    )(*results)
    return act, xg.T, wg, bg, gg.reshape(F)


def solution(mesh):
    in_specs = (P("row", "col"), P("col"), P("row", "col"), P("col"), P("row", "col"))
    out_specs = (P("row", "col"), P("row", "col"), P("row", "col"), P("col"), P("col"))
    return jax.shard_map(body, mesh=mesh, in_specs=in_specs, out_specs=out_specs, check_vma=False)
```

```python
import functools

import jax
import jax.numpy as jnp
from jax import lax
from jax.experimental import pallas as pl
from jax.experimental.pallas import tpu as pltpu
from jax.sharding import PartitionSpec as P

D = 6144
F = 192
T = 128
K = 768
G = 4
ROWS = T // G
MESH = pl.DeviceIdType.MESH
F32 = jnp.float32
BF16 = jnp.bfloat16
SQRT_HALF = 0.7071067811865476
INV_SQRT_2PI = 0.3989422804014327


def split3(row):
    hi = row.astype(BF16).astype(F32)
    rest = row - hi
    mid = rest.astype(BF16).astype(F32)
    low = rest - mid
    at = lax.broadcasted_iota(jnp.int32, (8, row.shape[1]), 0)
    rows = jnp.where(at == 0, hi, jnp.where(at == 1, mid, jnp.where(at == 2, low, 0.0)))
    return rows.astype(BF16)


def dot_nt(a, b):
    return lax.dot_general(a, b, (((1,), (1,)), ((), ())), preferred_element_type=F32)


def kernel(
    tok_hbm, gain_hbm, w_hbm, bias_hbm, cot_hbm,
    act_hbm, xg_hbm, wg_hbm, bg_hbm, gg_hbm,
    tok_ref, gain_ref, w_ref, bias_ref, cot_ref,
    normt, gaint, gaincol, stat1, stat2, zstat, xb, xn, part, pre, pg,
    rs_out, rs_in, ce_out, ce_in, ra_out, ra_in, home_out, home_in, dots, own,
    wz, gz_out, gz, act_ref, xg_ref, wg_ref, bg_ref, gg_ref,
    in_s, out_s, s1_s, s1_r, s2_s, s2_r, sh_s, sh_r, xa_s, xa_r, xb_s, xb_r, xc_s, xc_r, zs_s, zs_r,
    wz_s, wz_r, gz_s, gz_r, rs_s, rs_r, ag_s, ag_r, ce_s, ce_r, ra_s, ra_r, hm_s, hm_r,
):
    loads = [
        pltpu.make_async_copy(src, dst, in_s.at[i])
        for i, (src, dst) in enumerate([
            (tok_hbm, tok_ref), (gain_hbm, gain_ref), (w_hbm, w_ref), (bias_hbm, bias_ref), (cot_hbm, cot_ref),
        ])
    ]
    for load in loads:
        load.start()

    r = lax.axis_index("row")
    c = lax.axis_index("col")
    y = c // 8
    x = (c // 2) % 4
    e = c % 2
    a = (1 - e) * x + e * y
    b = (1 - e) * y + e * x

    def at(z, yy, xx, ee):
        return (z, (yy * 4 + xx) * 2 + ee)

    def place(z, aa, bb, ee):
        return at(z, (1 - ee) * bb + ee * aa, (1 - ee) * aa + ee * bb, ee)

    def zpeer(j):
        return at((r + j) % 8, y, x, e)

    def apeer(j):
        return place(r, (a + j) % 4, b, e)

    def bpeer(j):
        return place(r, a, (b + j) % 4, e)

    core = at(r, y, x, 1 - e)
    def turn(z):
        return (z // 2) % 2 + 2 * (1 - z % 2)

    def gatherer(k, bb, ee):
        z = c // 4
        return place(z, (k + 4 - turn(z)) % 4, bb, ee)

    my_k = (a + turn(r)) % 4
    my_q = 2 * b + e
    mine = pl.ds(pl.multiple_of(my_k * F, F), F)

    def holder(q):
        return (q, 4 * r + my_k)

    peers = [holder((r + j) % 8) for j in (4, 3, 5, 2, 6, 1, 7, 0)]
    peers += [gatherer(c % 4, bb, ee) for bb in range(4) for ee in range(2)]
    peers += [zpeer(j) for j in (4, 3, 5, 2, 6, 1, 7)]
    peers += [apeer(j) for j in (2, 1, 3)] + [bpeer(j) for j in (2, 1, 3)] + [core]
    barrier = pltpu.get_barrier_semaphore()
    for peer in peers:
        pl.semaphore_signal(barrier, inc=1, device_id=peer, device_id_type=MESH)

    pl.semaphore_wait(barrier, len(peers))

    def send(src, dst, ssem, rsem, to):
        return pltpu.make_async_remote_copy(
            src_ref=src, dst_ref=dst, send_sem=ssem, recv_sem=rsem, device_id=to, device_id_type=MESH
        )

    def arrived(dst, ssem, rsem):
        send(dst, dst, ssem, rsem, core).wait_recv()

    pending = []

    def go(src, dst, ssem, rsem, to):
        copy = send(src, dst, ssem, rsem, to)
        copy.start()
        pending.append(copy)

    def plane_gather(tiles, ssem, rsem):
        mine = (e * 4 + b) * 4
        for j in (1, 2, 3):
            ref = tiles.at[mine + a]
            go(ref, ref, ssem.at[j - 1], rsem.at[j - 1], apeer(j))
        yield
        for j in (1, 2, 3):
            arrived(tiles.at[mine + (a + 4 - j) % 4], ssem.at[j - 1], rsem.at[j - 1])
        for j in (1, 2, 3):
            ref = tiles.at[pl.ds(mine, 4)]
            go(ref, ref, ssem.at[j + 2], rsem.at[j + 2], bpeer(j))
        yield
        for j in (1, 2, 3):
            ref = tiles.at[pl.ds((e * 4 + (b + 4 - j) % 4) * 4, 4)]
            arrived(ref, ssem.at[j + 2], rsem.at[j + 2])
        ref = tiles.at[pl.ds(e * 16, 16)]
        go(ref, ref, ssem.at[6], rsem.at[6], core)
        yield
        arrived(tiles.at[pl.ds((1 - e) * 16, 16)], ssem.at[6], rsem.at[6])
        yield

    loads[0].wait()
    owner = gatherer(c % 4, r // 2, r % 2)
    go(tok_ref, xb.at[r, pl.ds(pl.multiple_of((c % 4) * F, F), F)], sh_s, sh_r, owner)

    loads[1].wait()
    xt = tok_ref[...].astype(F32)
    total = jnp.sum(xt, axis=0, keepdims=True)
    dev = xt - total / F
    squares = jnp.sum(dev * dev, axis=0, keepdims=True)
    slot = (e * 4 + b) * 4 + a
    stat1[slot] = jnp.zeros((8, T), F32)
    stat1[slot, 0:1, :] = total
    stat1[slot, 1:2, :] = squares
    stat1[slot, 2:3, :] = gain_ref[:, 0:128]
    stat1[slot, 3:4, 0:64] = gain_ref[:, 128:192]
    gather = plane_gather(stat1, s1_s, s1_r)
    next(gather)

    def chunk(q, k):
        return xb.at[q, pl.ds(pl.multiple_of(k * F, F), F)]

    def spread(k, i):
        for j in (2, 1, 3):
            n = i * 3 + j - 1
            go(chunk(my_q, k), chunk(my_q, k), xb_s.at[n], xb_r.at[n], bpeer(j))

    next(gather)
    ref = chunk(my_q, my_k)
    arrived(ref, sh_s, sh_r)
    for j in (2, 1, 3):
        go(ref, ref, xa_s.at[j - 1], xa_r.at[j - 1], apeer(j))
    spread(my_k, 0)
    next(gather)
    next(gather)
    sums = stat1[:, 0, :]
    mean = jnp.sum(sums, axis=0, keepdims=True) / D
    apart = sums / F - mean
    var = (
        jnp.sum(stat1[:, 1, :], axis=0, keepdims=True)
        + F * jnp.sum(apart * apart, axis=0, keepdims=True)
    ) / D
    rstd = lax.rsqrt(var + 1e-06)
    zstat[r] = jnp.zeros((8, T), F32)
    zstat[r, 0:1, :] = mean
    zstat[r, 1:2, :] = rstd
    for j in range(1, 8):
        go(zstat.at[r], zstat.at[r], zs_s.at[j - 1], zs_r.at[j - 1], zpeer(j))
    for j in (1, 3, 2):
        k = (my_k + 4 - j) % 4
        arrived(chunk(my_q, k), xa_s.at[j - 1], xa_r.at[j - 1])
        spread(k, j)
    go(xb.at[my_q], xb.at[my_q], xc_s.at[0], xc_r.at[0], core)
    for j in (1, 3, 2):
        q = 2 * ((b + 4 - j) % 4) + e
        for i in range(4):
            n = i * 3 + j - 1
            arrived(chunk(q, (my_k + 4 - i) % 4), xb_s.at[n], xb_r.at[n])
        go(xb.at[q], xb.at[q], xc_s.at[j], xc_r.at[j], core)
    grows = []
    for k in range(4):
        col = 4 * r + k
        cy, cx, ce = col // 8, (col // 2) % 4, col % 2
        gslot = (ce * 4 + (1 - ce) * cy + ce * cx) * 4 + (1 - ce) * cx + ce * cy
        grow = jnp.concatenate([stat1[gslot, 2:3, :], stat1[gslot, 3:4, 0:64]], axis=1)
        gaincol[k * F:(k + 1) * F, :] = jnp.broadcast_to(grow, (T, F)).T
        grows.append(split3(grow))
    loads[2].wait()
    gaint[...] = jnp.broadcast_to(gain_ref[...], (T, F)).T
    normt[...] = (xt - mean) * rstd
    wbar = jnp.zeros((8, K), F32)
    for k in range(4):
        wbar += jnp.dot(grows[k], w_ref[k * F:(k + 1) * F, :], preferred_element_type=F32)
    wz[r] = jnp.sum(wbar, axis=0, keepdims=True)
    for j in range(1, 8):
        go(wz.at[r], wz.at[r], wz_s.at[j - 1], wz_r.at[j - 1], zpeer(j))
    for j in range(1, 8):
        arrived(zstat.at[(r + 8 - j) % 8], zs_s.at[j - 1], zs_r.at[j - 1])
    for j in (0, 1, 3, 2):
        q = 2 * ((a + 4 - j) % 4) + 1 - e
        arrived(xb.at[q], xc_s.at[j], xc_r.at[j])

    def product(i, carry):
        odd = i % 2
        q = (r + (1 - odd) * (4 + i // 2) + odd * (3 - i // 2)) % 8
        for k in range(4):
            rows = slice(k * F, (k + 1) * F)
            normed = (xb[q, rows, :].astype(F32) - zstat[q, 0:1, :]) * zstat[q, 1:2, :]
            xn[q, rows, :] = (normed * gaincol[rows, :]).astype(BF16)
        part[q] = jnp.dot(xn[q].T, w_ref[...], preferred_element_type=F32)
        return carry

    def slot_of(way, s, g):
        return (way * 4 + s) * G + g

    def rows_of(g):
        return pl.ds(g * ROWS, ROWS)

    def ahead(way):
        return zpeer(1) if way == 0 else zpeer(7)

    def rs_step(s, g, ways):
        for way in ways:
            first = 0 if way == g % 2 else 1
            if s < first:
                continue
            q = (r + 4 - s) % 8 if way == 0 else (r + 4 + s) % 8
            value = part[q, rows_of(g), :]
            n = slot_of(way, s, g)
            if s > first:
                m = slot_of(way, s - 1, g)
                arrived(rs_in.at[m], rs_s.at[m], rs_r.at[m])
                value = value + rs_in[m].astype(F32)
            rs_out[n] = value.astype(BF16)
            go(rs_out.at[n], rs_in.at[n], rs_s.at[n], rs_r.at[n], ahead(way))

    def ag_step(t, g):
        for way in (g % 2, 1 - g % 2):
            if t == 4 and way != g % 2:
                continue
            q = (r + 9 - t) % 8 if way == 0 else (r + t - 1) % 8
            ref = pg.at[q, rows_of(g)]
            n = slot_of(way, t - 1, g)
            if t > 1:
                m = slot_of(way, t - 2, g)
                arrived(ref, ag_s.at[m], ag_r.at[m])
            go(ref, ref, ag_s.at[n], ag_r.at[n], ahead(way))

    def ag_last(t, g):
        way = g % 2 if t == 4 else 1 - g % 2
        q = (r + 8 - t) % 8 if way == 0 else (r + t) % 8
        m = slot_of(way, t - 1, g)
        arrived(pg.at[q, rows_of(g)], ag_s.at[m], ag_r.at[m])

    lax.fori_loop(0, 1, product, 0)
    for g in range(G):
        rs_step(0, g, (g % 2,))
    lax.fori_loop(1, 3, product, 0)
    for g in range(G):
        rs_step(1, g, (1 - g % 2,))
    lax.fori_loop(3, 8, product, 0)
    for g in range(G):
        rs_step(1, g, (g % 2,))
    for s in (2, 3):
        for g in range(G):
            rs_step(s, g, (g % 2, 1 - g % 2))
    loads[3].wait()
    loads[4].wait()
    bias = bias_ref[...].reshape(1, K)

    for g in range(G):
        rows = rows_of(g)
        raw = part[r, rows, :]
        for way in (g % 2, 1 - g % 2):
            m = slot_of(way, 3, g)
            arrived(rs_in.at[m], rs_s.at[m], rs_r.at[m])
            raw = raw + rs_in[m].astype(F32)
        v = raw + bias
        phi = 0.5 * (1.0 + lax.erf(v * SQRT_HALF))
        act_ref[rows, :] = (v * phi).astype(BF16)
        slope = phi + v * (INV_SQRT_2PI * jnp.exp(-0.5 * v * v))
        grad = (cot_ref[rows, :].astype(F32) * slope).astype(BF16)
        pg[r, rows, :] = grad
        ag_step(1, g)
        pre[rows, :] = jnp.broadcast_to(
            jnp.sum(grad.astype(F32) * raw, axis=1, keepdims=True), (ROWS, T)
        )
    stores = [
        pltpu.make_async_copy(src, dst, out_s.at[i])
        for i, (src, dst) in enumerate([
            (act_ref, act_hbm), (xg_ref, xg_hbm),
            (wg_ref.at[0:256], wg_hbm.at[0:256]), (wg_ref.at[256:512], wg_hbm.at[256:512]),
            (wg_ref.at[512:768], wg_hbm.at[512:768]), (bg_ref, bg_hbm), (gg_ref, gg_hbm),
        ])
    ]
    stores[0].start()
    for j in range(1, 8):
        arrived(wz.at[(r + 8 - j) % 8], wz_s.at[j - 1], wz_r.at[j - 1])
    wsum = split3(jnp.sum(wz[...], axis=0))

    swap = (r + e) % 2
    dots[...] = jnp.zeros((F, T), F32)

    def pair(p, even, odd):
        q = (r + 8 + (1 - swap) * even + swap * odd) % 8
        q_other = (r + 8 + (1 - swap) * odd + swap * even) % 8
        both = dot_nt(w_ref[...], jnp.concatenate([pg[q_other], pg[q]], axis=0))
        ce_out[p] = both[:, :T].astype(BF16)
        go(ce_out.at[p], ce_in.at[p], ce_s.at[p], ce_r.at[p], core)
        own[p] = both[:, T:]
        yield
        arrived(ce_in.at[p], ce_s.at[p], ce_r.at[p])
        for j in (2, 1, 3):
            k = (my_k + j) % 4
            rows = pl.ds(pl.multiple_of(k * F, F), F)
            n = p * 3 + j - 1
            ra_out[n] = (own[p, rows, :] + ce_in[p, rows, :].astype(F32)).astype(BF16)
            go(ra_out.at[n], ra_in.at[n], ra_s.at[n], ra_r.at[n], apeer(j))
        value = own[p, mine, :] + ce_in[p, mine, :].astype(F32)
        yield
        for j in (1, 3, 2):
            n = p * 3 + j - 1
            arrived(ra_in.at[n], ra_s.at[n], ra_r.at[n])
            value = value + ra_in[n].astype(F32)
        home_out[p] = value.astype(BF16)
        go(home_out.at[p], home_in.at[b], hm_s.at[p], hm_r.at[b], holder(q))
        raw = xb[q, mine, :].astype(F32)
        dots[...] += value * ((raw - zstat[q, 0:1, :]) * zstat[q, 1:2, :])
        yield

    def ag_all(t):
        for g in range(G):
            ag_step(t, g)

    second_col = pre[...].T[0:1, :]
    first = jnp.sum(dot_nt(wsum, pg[r]), axis=0, keepdims=True)
    stat2[slot] = jnp.zeros((8, T), F32)
    stat2[slot, 0:1, :] = first
    stat2[slot, 1:2, :] = second_col
    gather = plane_gather(stat2, s2_s, s2_r)
    next(gather)
    ag_all(2)
    next(gather)
    pairs = [pair(0, 0, 1), pair(1, 2, -1), pair(2, -2, 3), pair(3, 4, -3)]
    next(pairs[0])
    ag_all(3)
    next(gather)
    next(pairs[0])
    next(pairs[1])
    ag_all(4)
    next(gather)
    next(pairs[0])
    next(pairs[1])
    for g in range(G):
        ag_last(3, g)
    next(pairs[2])
    next(pairs[1])
    for g in range(G):
        ag_last(4, g)
    next(pairs[3])
    next(pairs[2])
    next(pairs[3])

    def weight(i):
        rows = slice(i * 256, (i + 1) * 256)
        lhs = jnp.concatenate([xn[q, rows, :] for q in range(8)], axis=1)
        wg_ref[rows, :] = jnp.dot(lhs, pg[...].reshape(8 * T, K), preferred_element_type=F32)
        stores[2 + i].start()

    weight(0)
    next(pairs[2])
    next(pairs[3])
    row = jnp.sum(dots[...].T, axis=0, keepdims=True)
    gz_out[0:1, :] = row[:, 0:128]
    gz_out[1:2, :] = jnp.concatenate([row[:, 128:192], jnp.zeros((1, 64), F32)], axis=1)
    for q in range(8):
        go(gz_out.at[0:2], gz.at[e * 4 + b, 0:2], gz_s.at[q], gz_r.at[e * 4 + b], holder(q))

    weight(1)
    weight(2)
    for copy in pending[:-13]:
        copy.wait_send()
    del pending[:-13]
    ones = jnp.ones((16, 8 * T), BF16)
    bg_ref[...] = jnp.dot(ones, pg[...].reshape(8 * T, K), preferred_element_type=F32)[0:1, :].reshape(K)
    stores[5].start()

    first = jnp.sum(stat2[:, 0, :], axis=0, keepdims=True) / D
    second = jnp.sum(stat2[:, 1, :], axis=0, keepdims=True) / D
    total = jnp.zeros((F, T), F32)
    for n in range(4):
        arrived(home_in.at[n], hm_s.at[0], hm_r.at[n])
        total = total + home_in[n].astype(F32)
    g = total * gaint[...]
    xg_ref[...] = (rstd * (g - first - normt[...] * second)).astype(BF16)
    stores[1].start()
    for n in range(8):
        arrived(gz.at[n, 0:2], gz_s.at[0], gz_r.at[n])
    row = jnp.sum(gz[:, 0:2, :], axis=0)
    gg_ref[...] = jnp.concatenate([row[0:1, :], row[1:2, 0:64]], axis=1)
    stores[6].start()

    for copy in stores:
        copy.wait()
    for copy in pending:
        copy.wait_send()

def store(*refs):
    ins, outs, held = refs[:5], refs[5:10], refs[10:15]
    in_sem, out_sem = refs[15:]
    rows = K // 8
    parts = []
    for i in range(8):
        at = pl.ds(i * rows, rows)
        parts.append((ins[2].at[at], held[2].at[at], outs[2].at[at]))
    parts += [(ins[i], held[i], outs[i]) for i in (0, 1, 3, 4)]
    loads = [pltpu.make_async_copy(src, mid, in_sem.at[i]) for i, (src, mid, _) in enumerate(parts)]
    stores = [pltpu.make_async_copy(mid, dst, out_sem.at[i]) for i, (_, mid, dst) in enumerate(parts)]
    for load in loads:
        load.start()
    for load, copy in zip(loads, stores):
        load.wait()
        copy.start()
    for copy in stores:
        copy.wait()


def body(tokens, norm_gain, up_weight, up_bias, cotangent):
    def vmem(shape, dtype):
        return pltpu.VMEM(shape, dtype)

    def sems(*shape):
        return pltpu.SemaphoreType.DMA(shape)

    scratch = [
        vmem((F, T), BF16), vmem((1, F), F32), vmem((K, K), BF16), vmem((K,), F32), vmem((T, K), BF16),
        vmem((F, T), F32), vmem((F, T), F32), vmem((K, T), F32),
        vmem((32, 8, T), F32), vmem((32, 8, T), F32), vmem((8, 8, T), F32),
        vmem((8, K, T), BF16), vmem((8, K, T), BF16), vmem((8, T, K), F32), vmem((T, T), F32), vmem((8, T, K), BF16),
        vmem((8 * G, ROWS, K), BF16), vmem((8 * G, ROWS, K), BF16),
        vmem((4, K, T), BF16), vmem((4, K, T), BF16),
        vmem((12, F, T), BF16), vmem((12, F, T), BF16),
        vmem((4, F, T), BF16), vmem((4, F, T), BF16), vmem((F, T), F32), vmem((4, K, T), F32),
        vmem((8, 1, K), F32), vmem((8, T), F32), vmem((8, 8, T), F32),
        vmem((T, K), BF16), vmem((F, T), BF16), vmem((K, K), F32), vmem((K,), F32), vmem((1, F), F32),
    ]
    scratch += [
        sems(5), sems(7), sems(7), sems(7), sems(7), sems(7), sems(), sems(), sems(3), sems(3), sems(12), sems(12),
        sems(4), sems(4), sems(7), sems(7), sems(7), sems(7), sems(8), sems(8),
        sems(8 * G), sems(8 * G), sems(8 * G), sems(8 * G),
        sems(4), sems(4), sems(12), sems(12), sems(4), sems(4),
    ]
    anywhere = pl.BlockSpec(memory_space=pl.ANY)
    shapes = [
        jax.ShapeDtypeStruct((T, K), BF16),
        jax.ShapeDtypeStruct((F, T), BF16),
        jax.ShapeDtypeStruct((K, K), F32),
        jax.ShapeDtypeStruct((K,), F32),
        jax.ShapeDtypeStruct((1, F), F32),
    ]
    results = pl.pallas_call(
        kernel,
        out_shape=shapes,
        in_specs=[pl.BlockSpec(memory_space=pltpu.HBM)] * 5,
        out_specs=[anywhere] * 5,
        scratch_shapes=scratch,
        compiler_params=pltpu.CompilerParams(
            collective_id=0, has_side_effects=True, vmem_limit_bytes=58 * 2**20
        ),
        name="mlp_up",
    )(tokens.T, norm_gain.reshape(1, F), up_weight, up_bias, cotangent)
    act, xg, wg, bg, gg = pl.pallas_call(
        store,
        out_shape=shapes,
        in_specs=[anywhere] * 5,
        out_specs=[anywhere] * 5,
        scratch_shapes=[vmem(t.shape, t.dtype) for t in shapes] + [sems(12), sems(12)],
        compiler_params=pltpu.CompilerParams(vmem_limit_bytes=60 * 2**20),
        name="store",
    )(*results)
    return act, xg.T, wg, bg, gg.reshape(F)


def solution(mesh):
    in_specs = (P("row", "col"), P("col"), P("row", "col"), P("col"), P("row", "col"))
    out_specs = (P("row", "col"), P("row", "col"), P("row", "col"), P("col"), P("col"))
    return jax.shard_map(body, mesh=mesh, in_specs=in_specs, out_specs=out_specs, check_vma=False)
```

```python
import functools

import jax
import jax.numpy as jnp
from jax import lax
from jax.experimental import pallas as pl
from jax.experimental.pallas import tpu as pltpu
from jax.sharding import PartitionSpec as P

D = 6144
F = 192
T = 128
K = 768
G = 4
ROWS = T // G
MESH = pl.DeviceIdType.MESH
F32 = jnp.float32
BF16 = jnp.bfloat16
SQRT_HALF = 0.7071067811865476
INV_SQRT_2PI = 0.3989422804014327


def split3(row):
    hi = row.astype(BF16).astype(F32)
    rest = row - hi
    mid = rest.astype(BF16).astype(F32)
    low = rest - mid
    at = lax.broadcasted_iota(jnp.int32, (8, row.shape[1]), 0)
    rows = jnp.where(at == 0, hi, jnp.where(at == 1, mid, jnp.where(at == 2, low, 0.0)))
    return rows.astype(BF16)


def dot_nt(a, b):
    return lax.dot_general(a, b, (((1,), (1,)), ((), ())), preferred_element_type=F32)


def kernel(
    tok_hbm, gain_hbm, w_hbm, bias_hbm, cot_hbm,
    act_hbm, xg_hbm, wg_hbm, bg_hbm, gg_hbm,
    tok_ref, gain_ref, w_ref, bias_ref, cot_ref,
    normt, gaint, gaincol, stat1, stat2, zstat, xb, xn, part, pre, pg,
    rs_out, rs_in, ce_out, ce_in, ra_out, ra_in, home_out, home_in, dots, own,
    wz, gz_out, gz, act_ref, xg_ref, wg_ref, bg_ref, gg_ref,
    in_s, out_s, s1_s, s1_r, s2_s, s2_r, sh_s, sh_r, xa_s, xa_r, xb_s, xb_r, xc_s, xc_r, zs_s, zs_r,
    wz_s, wz_r, gz_s, gz_r, rs_s, rs_r, ag_s, ag_r, ce_s, ce_r, ra_s, ra_r, hm_s, hm_r,
):
    loads = [
        pltpu.make_async_copy(src, dst, in_s.at[i])
        for i, (src, dst) in enumerate([
            (tok_hbm, tok_ref), (gain_hbm, gain_ref), (w_hbm, w_ref), (bias_hbm, bias_ref), (cot_hbm, cot_ref),
        ])
    ]
    for load in loads:
        load.start()

    r = lax.axis_index("row")
    c = lax.axis_index("col")
    y = c // 8
    x = (c // 2) % 4
    e = c % 2
    a = (1 - e) * x + e * y
    b = (1 - e) * y + e * x

    def at(z, yy, xx, ee):
        return (z, (yy * 4 + xx) * 2 + ee)

    def place(z, aa, bb, ee):
        return at(z, (1 - ee) * bb + ee * aa, (1 - ee) * aa + ee * bb, ee)

    def zpeer(j):
        return at((r + j) % 8, y, x, e)

    def apeer(j):
        return place(r, (a + j) % 4, b, e)

    def bpeer(j):
        return place(r, a, (b + j) % 4, e)

    core = at(r, y, x, 1 - e)
    def turn(z):
        return (z // 2) % 2 + 2 * (1 - z % 2)

    def gatherer(k, bb, ee):
        z = c // 4
        return place(z, (k + 4 - turn(z)) % 4, bb, ee)

    my_k = (a + turn(r)) % 4
    my_q = 2 * b + e
    mine = pl.ds(pl.multiple_of(my_k * F, F), F)

    def holder(q):
        return (q, 4 * r + my_k)

    peers = [zpeer(j) for j in range(1, 8)]
    peers += [apeer(j) for j in (1, 2, 3)] + [bpeer(j) for j in (1, 2, 3)] + [core]
    peers += [holder(q) for q in range(8)]
    peers += [gatherer(c % 4, bb, ee) for bb in range(4) for ee in range(2)]
    barrier = pltpu.get_barrier_semaphore()
    for peer in peers:
        pl.semaphore_signal(barrier, inc=1, device_id=peer, device_id_type=MESH)

    pl.semaphore_wait(barrier, len(peers))

    def send(src, dst, ssem, rsem, to):
        return pltpu.make_async_remote_copy(
            src_ref=src, dst_ref=dst, send_sem=ssem, recv_sem=rsem, device_id=to, device_id_type=MESH
        )

    def arrived(dst, ssem, rsem):
        send(dst, dst, ssem, rsem, core).wait_recv()

    pending = []

    def go(src, dst, ssem, rsem, to):
        copy = send(src, dst, ssem, rsem, to)
        copy.start()
        pending.append(copy)

    def plane_gather(tiles, ssem, rsem):
        mine = (e * 4 + b) * 4
        for j in (1, 2, 3):
            ref = tiles.at[mine + a]
            go(ref, ref, ssem.at[j - 1], rsem.at[j - 1], apeer(j))
        yield
        for j in (1, 2, 3):
            arrived(tiles.at[mine + (a + 4 - j) % 4], ssem.at[j - 1], rsem.at[j - 1])
        for j in (1, 2, 3):
            ref = tiles.at[pl.ds(mine, 4)]
            go(ref, ref, ssem.at[j + 2], rsem.at[j + 2], bpeer(j))
        yield
        for j in (1, 2, 3):
            ref = tiles.at[pl.ds((e * 4 + (b + 4 - j) % 4) * 4, 4)]
            arrived(ref, ssem.at[j + 2], rsem.at[j + 2])
        ref = tiles.at[pl.ds(e * 16, 16)]
        go(ref, ref, ssem.at[6], rsem.at[6], core)
        yield
        arrived(tiles.at[pl.ds((1 - e) * 16, 16)], ssem.at[6], rsem.at[6])
        yield

    loads[0].wait()
    owner = gatherer(c % 4, r // 2, r % 2)
    go(tok_ref, xb.at[r, pl.ds(pl.multiple_of((c % 4) * F, F), F)], sh_s, sh_r, owner)

    loads[1].wait()
    xt = tok_ref[...].astype(F32)
    total = jnp.sum(xt, axis=0, keepdims=True)
    dev = xt - total / F
    squares = jnp.sum(dev * dev, axis=0, keepdims=True)
    slot = (e * 4 + b) * 4 + a
    stat1[slot] = jnp.zeros((8, T), F32)
    stat1[slot, 0:1, :] = total
    stat1[slot, 1:2, :] = squares
    stat1[slot, 2:3, :] = gain_ref[:, 0:128]
    stat1[slot, 3:4, 0:64] = gain_ref[:, 128:192]
    gather = plane_gather(stat1, s1_s, s1_r)
    next(gather)

    def chunk(q, k):
        return xb.at[q, pl.ds(pl.multiple_of(k * F, F), F)]

    def spread(k, i):
        for j in (2, 1, 3):
            n = i * 3 + j - 1
            go(chunk(my_q, k), chunk(my_q, k), xb_s.at[n], xb_r.at[n], bpeer(j))

    next(gather)
    ref = chunk(my_q, my_k)
    arrived(ref, sh_s, sh_r)
    for j in (2, 1, 3):
        go(ref, ref, xa_s.at[j - 1], xa_r.at[j - 1], apeer(j))
    spread(my_k, 0)
    next(gather)
    next(gather)
    sums = stat1[:, 0, :]
    mean = jnp.sum(sums, axis=0, keepdims=True) / D
    apart = sums / F - mean
    var = (
        jnp.sum(stat1[:, 1, :], axis=0, keepdims=True)
        + F * jnp.sum(apart * apart, axis=0, keepdims=True)
    ) / D
    rstd = lax.rsqrt(var + 1e-06)
    zstat[r] = jnp.zeros((8, T), F32)
    zstat[r, 0:1, :] = mean
    zstat[r, 1:2, :] = rstd
    for j in range(1, 8):
        go(zstat.at[r], zstat.at[r], zs_s.at[j - 1], zs_r.at[j - 1], zpeer(j))
    for j in (1, 3, 2):
        k = (my_k + 4 - j) % 4
        arrived(chunk(my_q, k), xa_s.at[j - 1], xa_r.at[j - 1])
        spread(k, j)
    go(xb.at[my_q], xb.at[my_q], xc_s.at[0], xc_r.at[0], core)
    for j in (1, 3, 2):
        q = 2 * ((b + 4 - j) % 4) + e
        for i in range(4):
            n = i * 3 + j - 1
            arrived(chunk(q, (my_k + 4 - i) % 4), xb_s.at[n], xb_r.at[n])
        go(xb.at[q], xb.at[q], xc_s.at[j], xc_r.at[j], core)
    grows = []
    for k in range(4):
        col = 4 * r + k
        cy, cx, ce = col // 8, (col // 2) % 4, col % 2
        gslot = (ce * 4 + (1 - ce) * cy + ce * cx) * 4 + (1 - ce) * cx + ce * cy
        grow = jnp.concatenate([stat1[gslot, 2:3, :], stat1[gslot, 3:4, 0:64]], axis=1)
        gaincol[k * F:(k + 1) * F, :] = jnp.broadcast_to(grow, (T, F)).T
        grows.append(split3(grow))
    loads[2].wait()
    for j in range(1, 8):
        arrived(zstat.at[(r + 8 - j) % 8], zs_s.at[j - 1], zs_r.at[j - 1])
    for j in (0, 1, 3, 2):
        q = 2 * ((a + 4 - j) % 4) + 1 - e
        arrived(xb.at[q], xc_s.at[j], xc_r.at[j])

    def product(i, carry):
        odd = i % 2
        q = (r + (1 - odd) * (4 + i // 2) + odd * (3 - i // 2)) % 8
        for k in range(4):
            rows = slice(k * F, (k + 1) * F)
            normed = (xb[q, rows, :].astype(F32) - zstat[q, 0:1, :]) * zstat[q, 1:2, :]
            xn[q, rows, :] = (normed * gaincol[rows, :]).astype(BF16)
        part[q] = jnp.dot(xn[q].T, w_ref[...], preferred_element_type=F32)
        return carry

    def slot_of(way, s, g):
        return (way * 4 + s) * G + g

    def rows_of(g):
        return pl.ds(g * ROWS, ROWS)

    def ahead(way):
        return zpeer(1) if way == 0 else zpeer(7)

    def rs_step(s, g, ways):
        for way in ways:
            first = 0 if way == g % 2 else 1
            if s < first:
                continue
            q = (r + 4 - s) % 8 if way == 0 else (r + 4 + s) % 8
            value = part[q, rows_of(g), :]
            n = slot_of(way, s, g)
            if s > first:
                m = slot_of(way, s - 1, g)
                arrived(rs_in.at[m], rs_s.at[m], rs_r.at[m])
                value = value + rs_in[m].astype(F32)
            rs_out[n] = value.astype(BF16)
            go(rs_out.at[n], rs_in.at[n], rs_s.at[n], rs_r.at[n], ahead(way))

    def ag_step(t, g):
        for way in (g % 2, 1 - g % 2):
            if t == 4 and way != g % 2:
                continue
            q = (r + 9 - t) % 8 if way == 0 else (r + t - 1) % 8
            ref = pg.at[q, rows_of(g)]
            n = slot_of(way, t - 1, g)
            if t > 1:
                m = slot_of(way, t - 2, g)
                arrived(ref, ag_s.at[m], ag_r.at[m])
            go(ref, ref, ag_s.at[n], ag_r.at[n], ahead(way))

    def ag_last(t, g):
        way = g % 2 if t == 4 else 1 - g % 2
        q = (r + 8 - t) % 8 if way == 0 else (r + t) % 8
        m = slot_of(way, t - 1, g)
        arrived(pg.at[q, rows_of(g)], ag_s.at[m], ag_r.at[m])

    lax.fori_loop(0, 1, product, 0)
    for g in range(G):
        rs_step(0, g, (g % 2,))
    lax.fori_loop(1, 3, product, 0)
    for g in range(G):
        rs_step(1, g, (1 - g % 2,))
    lax.fori_loop(3, 8, product, 0)
    for g in range(G):
        rs_step(1, g, (g % 2,))
    gaint[...] = jnp.broadcast_to(gain_ref[...], (T, F)).T
    normt[...] = (xt - mean) * rstd
    wbar = jnp.zeros((8, K), F32)
    for k in range(4):
        wbar += jnp.dot(grows[k], w_ref[k * F:(k + 1) * F, :], preferred_element_type=F32)
    wz[r] = jnp.sum(wbar, axis=0, keepdims=True)
    for j in range(1, 8):
        go(wz.at[r], wz.at[r], wz_s.at[j - 1], wz_r.at[j - 1], zpeer(j))
    for s in (2, 3):
        for g in range(G):
            rs_step(s, g, (g % 2, 1 - g % 2))
    loads[3].wait()
    loads[4].wait()
    bias = bias_ref[...].reshape(1, K)

    for g in range(G):
        rows = rows_of(g)
        raw = part[r, rows, :]
        for way in (g % 2, 1 - g % 2):
            m = slot_of(way, 3, g)
            arrived(rs_in.at[m], rs_s.at[m], rs_r.at[m])
            raw = raw + rs_in[m].astype(F32)
        v = raw + bias
        phi = 0.5 * (1.0 + lax.erf(v * SQRT_HALF))
        act_ref[rows, :] = (v * phi).astype(BF16)
        slope = phi + v * (INV_SQRT_2PI * jnp.exp(-0.5 * v * v))
        grad = (cot_ref[rows, :].astype(F32) * slope).astype(BF16)
        pg[r, rows, :] = grad
        ag_step(1, g)
        pre[rows, :] = jnp.broadcast_to(
            jnp.sum(grad.astype(F32) * raw, axis=1, keepdims=True), (ROWS, T)
        )
    stores = [
        pltpu.make_async_copy(src, dst, out_s.at[i])
        for i, (src, dst) in enumerate([
            (act_ref, act_hbm), (xg_ref, xg_hbm),
            (wg_ref.at[0:256], wg_hbm.at[0:256]), (wg_ref.at[256:512], wg_hbm.at[256:512]),
            (wg_ref.at[512:768], wg_hbm.at[512:768]), (bg_ref, bg_hbm), (gg_ref, gg_hbm),
        ])
    ]
    stores[0].start()
    for j in range(1, 8):
        arrived(wz.at[(r + 8 - j) % 8], wz_s.at[j - 1], wz_r.at[j - 1])
    wsum = split3(jnp.sum(wz[...], axis=0))

    swap = (r + e) % 2
    dots[...] = jnp.zeros((F, T), F32)

    def pair(p, even, odd):
        q = (r + 8 + (1 - swap) * even + swap * odd) % 8
        q_other = (r + 8 + (1 - swap) * odd + swap * even) % 8
        if p == 3:
            ce_out[p] = dot_nt(w_ref[...], pg[q_other]).astype(BF16)
            go(ce_out.at[p], ce_in.at[p], ce_s.at[p], ce_r.at[p], core)
            own[p] = dot_nt(w_ref[...], pg[q])
        else:
            both = dot_nt(w_ref[...], jnp.concatenate([pg[q_other], pg[q]], axis=0))
            ce_out[p] = both[:, :T].astype(BF16)
            go(ce_out.at[p], ce_in.at[p], ce_s.at[p], ce_r.at[p], core)
            own[p] = both[:, T:]
        yield
        arrived(ce_in.at[p], ce_s.at[p], ce_r.at[p])
        for j in (2, 1, 3):
            k = (my_k + j) % 4
            rows = pl.ds(pl.multiple_of(k * F, F), F)
            n = p * 3 + j - 1
            ra_out[n] = (own[p, rows, :] + ce_in[p, rows, :].astype(F32)).astype(BF16)
            go(ra_out.at[n], ra_in.at[n], ra_s.at[n], ra_r.at[n], apeer(j))
        value = own[p, mine, :] + ce_in[p, mine, :].astype(F32)
        yield
        for j in (1, 3, 2):
            n = p * 3 + j - 1
            arrived(ra_in.at[n], ra_s.at[n], ra_r.at[n])
            value = value + ra_in[n].astype(F32)
        home_out[p] = value.astype(BF16)
        go(home_out.at[p], home_in.at[b], hm_s.at[p], hm_r.at[b], holder(q))
        raw = xb[q, mine, :].astype(F32)
        dots[...] += value * ((raw - zstat[q, 0:1, :]) * zstat[q, 1:2, :])
        yield

    def ag_all(t):
        for g in range(G):
            ag_step(t, g)

    second_col = pre[...].T[0:1, :]
    first = jnp.sum(dot_nt(wsum, pg[r]), axis=0, keepdims=True)
    stat2[slot] = jnp.zeros((8, T), F32)
    stat2[slot, 0:1, :] = first
    stat2[slot, 1:2, :] = second_col
    gather = plane_gather(stat2, s2_s, s2_r)
    next(gather)
    ag_all(2)
    next(gather)
    pairs = [pair(0, 0, 1), pair(1, 2, -1), pair(2, -2, 3), pair(3, 4, -3)]
    next(pairs[0])
    ag_all(3)
    next(gather)
    next(pairs[0])
    next(pairs[1])
    ag_all(4)
    next(gather)
    next(pairs[0])
    next(pairs[1])
    for g in range(G):
        ag_last(3, g)
    next(pairs[2])
    next(pairs[1])
    for g in range(G):
        ag_last(4, g)
    next(pairs[3])
    next(pairs[2])
    next(pairs[3])

    def weight(i):
        rows = slice(i * 256, (i + 1) * 256)
        lhs = jnp.concatenate([xn[q, rows, :] for q in range(8)], axis=1)
        wg_ref[rows, :] = jnp.dot(lhs, pg[...].reshape(8 * T, K), preferred_element_type=F32)
        stores[2 + i].start()

    weight(0)
    next(pairs[2])
    next(pairs[3])
    row = jnp.sum(dots[...].T, axis=0, keepdims=True)
    gz_out[0:1, :] = row[:, 0:128]
    gz_out[1:2, :] = jnp.concatenate([row[:, 128:192], jnp.zeros((1, 64), F32)], axis=1)
    for q in range(8):
        go(gz_out.at[0:2], gz.at[e * 4 + b, 0:2], gz_s.at[q], gz_r.at[e * 4 + b], holder(q))

    weight(1)
    weight(2)
    for copy in pending[:-13]:
        copy.wait_send()
    del pending[:-13]
    ones = jnp.ones((16, 8 * T), BF16)
    bg_ref[...] = jnp.dot(ones, pg[...].reshape(8 * T, K), preferred_element_type=F32)[0:1, :].reshape(K)
    stores[5].start()

    first = jnp.sum(stat2[:, 0, :], axis=0, keepdims=True) / D
    second = jnp.sum(stat2[:, 1, :], axis=0, keepdims=True) / D
    total = jnp.zeros((F, T), F32)
    for n in range(4):
        arrived(home_in.at[n], hm_s.at[0], hm_r.at[n])
        total = total + home_in[n].astype(F32)
    g = total * gaint[...]
    xg_ref[...] = (rstd * (g - first - normt[...] * second)).astype(BF16)
    stores[1].start()
    for n in range(8):
        arrived(gz.at[n, 0:2], gz_s.at[0], gz_r.at[n])
    row = jnp.sum(gz[:, 0:2, :], axis=0)
    gg_ref[...] = jnp.concatenate([row[0:1, :], row[1:2, 0:64]], axis=1)
    stores[6].start()

    for copy in stores:
        copy.wait()
    for copy in pending:
        copy.wait_send()

def store(*refs):
    ins, outs, held = refs[:5], refs[5:10], refs[10:15]
    in_sem, out_sem = refs[15:]
    rows = K // 8
    parts = [(ins[i], held[i], outs[i]) for i in (0, 1, 3, 4)]
    for i in range(8):
        at = pl.ds(i * rows, rows)
        parts.append((ins[2].at[at], held[2].at[at], outs[2].at[at]))
    loads = [pltpu.make_async_copy(src, mid, in_sem.at[i]) for i, (src, mid, _) in enumerate(parts)]
    stores = [pltpu.make_async_copy(mid, dst, out_sem.at[i]) for i, (_, mid, dst) in enumerate(parts)]
    for load in loads:
        load.start()
    for load, copy in zip(loads, stores):
        load.wait()
        copy.start()
    for copy in stores:
        copy.wait()


def body(tokens, norm_gain, up_weight, up_bias, cotangent):
    def vmem(shape, dtype):
        return pltpu.VMEM(shape, dtype)

    def sems(*shape):
        return pltpu.SemaphoreType.DMA(shape)

    scratch = [
        vmem((F, T), BF16), vmem((1, F), F32), vmem((K, K), BF16), vmem((K,), F32), vmem((T, K), BF16),
        vmem((F, T), F32), vmem((F, T), F32), vmem((K, T), F32),
        vmem((32, 8, T), F32), vmem((32, 8, T), F32), vmem((8, 8, T), F32),
        vmem((8, K, T), BF16), vmem((8, K, T), BF16), vmem((8, T, K), F32), vmem((T, T), F32), vmem((8, T, K), BF16),
        vmem((8 * G, ROWS, K), BF16), vmem((8 * G, ROWS, K), BF16),
        vmem((4, K, T), BF16), vmem((4, K, T), BF16),
        vmem((12, F, T), BF16), vmem((12, F, T), BF16),
        vmem((4, F, T), BF16), vmem((4, F, T), BF16), vmem((F, T), F32), vmem((4, K, T), F32),
        vmem((8, 1, K), F32), vmem((8, T), F32), vmem((8, 8, T), F32),
        vmem((T, K), BF16), vmem((F, T), BF16), vmem((K, K), F32), vmem((K,), F32), vmem((1, F), F32),
    ]
    scratch += [
        sems(5), sems(7), sems(7), sems(7), sems(7), sems(7), sems(), sems(), sems(3), sems(3), sems(12), sems(12),
        sems(4), sems(4), sems(7), sems(7), sems(7), sems(7), sems(8), sems(8),
        sems(8 * G), sems(8 * G), sems(8 * G), sems(8 * G),
        sems(4), sems(4), sems(12), sems(12), sems(4), sems(4),
    ]
    anywhere = pl.BlockSpec(memory_space=pl.ANY)
    shapes = [
        jax.ShapeDtypeStruct((T, K), BF16),
        jax.ShapeDtypeStruct((F, T), BF16),
        jax.ShapeDtypeStruct((K, K), F32),
        jax.ShapeDtypeStruct((K,), F32),
        jax.ShapeDtypeStruct((1, F), F32),
    ]
    results = pl.pallas_call(
        kernel,
        out_shape=shapes,
        in_specs=[pl.BlockSpec(memory_space=pltpu.HBM)] * 5,
        out_specs=[anywhere] * 5,
        scratch_shapes=scratch,
        compiler_params=pltpu.CompilerParams(
            collective_id=0, has_side_effects=True, vmem_limit_bytes=58 * 2**20
        ),
        name="mlp_up",
    )(tokens.T, norm_gain.reshape(1, F), up_weight, up_bias, cotangent)
    act, xg, wg, bg, gg = pl.pallas_call(
        store,
        out_shape=shapes,
        in_specs=[anywhere] * 5,
        out_specs=[anywhere] * 5,
        scratch_shapes=[vmem(t.shape, t.dtype) for t in shapes] + [sems(12), sems(12)],
        compiler_params=pltpu.CompilerParams(vmem_limit_bytes=60 * 2**20),
        name="store",
    )(*results)
    return act, xg.T, wg, bg, gg.reshape(F)


def solution(mesh):
    in_specs = (P("row", "col"), P("col"), P("row", "col"), P("col"), P("row", "col"))
    out_specs = (P("row", "col"), P("row", "col"), P("row", "col"), P("col"), P("col"))
    return jax.shard_map(body, mesh=mesh, in_specs=in_specs, out_specs=out_specs, check_vma=False)
```
